512 devices in a mesh: dp: 64 (over z_lo, y, core), tensor: 8 (over x, z_hi).
Axes of the slice: x: 4, y: 8, z: 8 (z_hi: 2, z_lo: 4; z = z_hi * 4 + z_lo), core: 2. Of those that a mesh axis runs over, the one named last changes fastest.
Arguments:
- item_cache: bfloat16 [2048, 3584], P('dp', 'tensor'), may hold values from -0.5 to 0.5
- user_cache: bfloat16 [2048, 3584], P('dp', 'tensor'), may hold values from -0.5 to 0.5
- positive: int32 [2048], P('dp'), may hold values from 0 to 2047, each once
- attn_heads: bfloat16 [16384, 2048], P('dp', 'tensor'), may hold values from -6 to 6
- residual: bfloat16 [16384, 3584], P('dp'), may hold values from -2.390625 to 2.390625
- out_proj: bfloat16 [2048, 3584], P('tensor'), may hold values from -0.125 to 0.125
- norm_gain: float32 [3584], replicated, may hold values from 0.1 to 1.9
Outputs:
- loss_mean: float32 [], replicated
- item_grad: float32 [2048, 3584], P('dp', 'tensor')
- user_grad: float32 [2048, 3584], P('dp', 'tensor')
- head_grad: bfloat16 [16384, 2048], P('dp', 'tensor')
- weight_grad: float32 [2048, 3584], P('tensor', 'dp')
The draws below stay inside these ranges and needn't reach their ends.
All inputs are finite; a program needn't handle non-finite values.
Results may differ from the reference program's by a relative error of at most 0.0051.
Values may be sent and summed in bfloat16 or wider, within the bound.
No kernel may reach another device: no remote copies, remote signals or barrier semaphores. Data moves between devices by JAX's collectives and lax.ppermute only.
A program may use at most 64 MiB of HBM per device.

```python
import jax
import jax.numpy as jnp
from jax import lax

D = 3584
PAIRS_DEV = 32
GROUP = 8
SEQ = 32
PAIRS = 2048
TOKENS = 16384
HF = 2048
N_DP = 64


def rising_scale(key, start, ratio):
    row_pos = jnp.arange(PAIRS).astype(jnp.float32) / PAIRS
    jitter = jax.random.uniform(jax.random.fold_in(key, 7), (PAIRS, 1), jnp.float32, 0.7, 1.4)
    return start * jnp.power(ratio, row_pos)[:, None] * jitter


def draw_user_cache(key, part):
    key = jax.random.fold_in(key, 3)
    spread = 0.6 / jnp.sqrt(jnp.float32(D))
    values = jnp.clip(jax.random.normal(key, (PAIRS, D), jnp.float32) * spread, -0.5, 0.5)
    return values.astype(jnp.bfloat16)


def draw_item_cache(key, part):
    key = jax.random.fold_in(key, 2)
    scale_rows = rising_scale(key, 0.01, 20.0)
    values = jnp.clip(jax.random.normal(key, (PAIRS, D), jnp.float32) * scale_rows, -0.5, 0.5)
    return values.astype(jnp.bfloat16)


def steps_of(rng, dims, pieces, smallest, high):
    gain, own = 1.0, jax.random.fold_in(rng, 6)
    for dim, blocks in pieces:
        steps = jnp.exp(jax.random.uniform(jax.random.fold_in(own, dim), (blocks,), jnp.float32, smallest / len(pieces), high / len(pieces)))
        gain = gain * jnp.repeat(steps, dims[dim] // blocks).reshape([-1 if axis == dim else 1 for axis in range(len(dims))])
    return gain


def normal_values(stream_key, extent, deviation, limit, split=(), kind=jnp.bfloat16):
    values = deviation * jax.random.normal(stream_key, extent, jnp.float32)
    if split:
        values = values * steps_of(stream_key, extent, split, -0.22, 0.18)
    return jnp.clip(values, -limit, limit).astype(kind)


def setup_inputs(seed: int = 0) -> dict:
    key_of = jax.random.split(jax.random.key(seed), 8)
    item_cache = draw_item_cache(jax.random.fold_in(key_of[7], 71), 0)
    user_cache = draw_user_cache(jax.random.fold_in(key_of[7], 71), 0)
    positive = jax.random.permutation(key_of[2], PAIRS).astype(jnp.int32)
    attn_heads = normal_values(key_of[3], (TOKENS, HF), 1.0, 6.0, ((0, 64), (1, 8)))
    residual = normal_values(key_of[4], (TOKENS, D), 0.3, 2.390625, ((0, 64),))
    out_proj = normal_values(key_of[5], (HF, D), HF ** -0.5, 0.125, ((0, 8),))
    norm_gain = jnp.clip(1.0 + 0.18 * jax.random.normal(key_of[6], (D,), jnp.float32), 0.1, 1.9)
    return dict(item_cache=item_cache, user_cache=user_cache, positive=positive, attn_heads=attn_heads, residual=residual, out_proj=out_proj, norm_gain=norm_gain)


logit_scale = 50.0
norm_eps = 1e-06

def reference(item_cache, user_cache, positive, attn_heads, residual, out_proj, norm_gain):
    scores = jnp.dot(item_cache, user_cache.T, preferred_element_type=jnp.float32) * logit_scale
    maxima = lax.optimization_barrier(jnp.max(scores, axis=1, keepdims=True))
    log_total = maxima[:, 0] + jnp.log(lax.optimization_barrier(jnp.sum(jnp.exp(scores - maxima), axis=1)))
    columns = jnp.arange(PAIRS, dtype=jnp.int32)
    target = positive[:, None] == columns[None, :]
    picked = lax.optimization_barrier(jnp.sum(jnp.where(target, scores, jnp.float32(0.0)), axis=1))
    row_loss = log_total - picked
    loss_mean = jnp.mean(row_loss)
    grad_logits = (jnp.exp(scores - log_total[:, None]) - target.astype(jnp.float32)).astype(jnp.bfloat16)
    item_grad = jnp.dot(grad_logits, user_cache, preferred_element_type=jnp.float32) * logit_scale
    user_grad = jnp.dot(grad_logits.T, item_cache, preferred_element_type=jnp.float32) * logit_scale
    mixed = jnp.dot(attn_heads, out_proj, preferred_element_type=jnp.float32)
    hidden = residual.astype(jnp.float32) + mixed
    inverse = lax.rsqrt(lax.optimization_barrier(jnp.mean(hidden * hidden, axis=1, keepdims=True)) + norm_eps)
    chosen = item_grad.reshape(N_DP, PAIRS_DEV, D)[:, :GROUP]
    pooled = jnp.broadcast_to(chosen[:, :, None, :], (N_DP, GROUP, SEQ, D)).reshape(TOKENS, D) / SEQ
    upstream = norm_gain[None, :] * pooled
    inner = lax.optimization_barrier(jnp.sum(upstream * hidden, axis=1, keepdims=True)) / D
    stream_grad = (inverse * upstream - hidden * inverse * inverse * inverse * inner).astype(jnp.bfloat16)
    head_grad = jnp.dot(stream_grad, out_proj.T, preferred_element_type=jnp.float32).astype(jnp.bfloat16)
    weight_grad = jnp.dot(attn_heads.T, stream_grad, preferred_element_type=jnp.float32)
    return (loss_mean, item_grad, user_grad, head_grad, weight_grad)
```

```python
import jax
import jax.numpy as jnp
from jax import lax
from jax.sharding import Mesh, PartitionSpec as P

BF16 = jnp.bfloat16
F32 = jnp.float32
LOGIT_SCALE = 50.0
NORM_EPS = 1e-06
GROUP = 8
SEQ = 32
AXES = (("zl", 4), ("y", 8), ("c", 2), ("x", 4), ("zh", 2))
TENSOR = ("x", "zh")
PLANE = ("zl", "y")
DP = ("zl", "y", "c")
SWAP = ((0, 1), (1, 0))
N_T = 8
N_P = 32


def three_terms(value):
    high = lax.reduce_precision(value, 8, 7)
    rest = value - high
    middle = lax.reduce_precision(rest, 8, 7)
    low = lax.reduce_precision(rest - middle, 8, 7)
    return high.astype(BF16), middle.astype(BF16), low.astype(BF16)


def to_all(value, axes, count):
    return lax.all_to_all(jnp.broadcast_to(value[None], (count,) + value.shape), axes, 0, 0)


def dot(a, b, dims):
    return lax.dot_general(a, b, (dims, ((), ())), preferred_element_type=F32)


def per_device(item_cache, user_cache, positive, attn_heads, residual, out_proj, norm_gain):
    rows, feats = item_cache.shape
    width = out_proj.shape[1]
    tokens, heads = attn_heads.shape
    half = N_P * rows
    core = lax.axis_index("c")
    dp_index = lax.axis_index(DP)
    t_index = lax.axis_index(TENSOR)

    pair = jnp.concatenate([user_cache, item_cache], axis=1)
    pair_own = to_all(pair, PLANE, N_P).reshape(half, 2 * feats)
    pair_other = lax.ppermute(pair_own, "c", SWAP)
    users = (pair_own[:, :feats], pair_other[:, :feats])
    items = (pair_own[:, feats:], pair_other[:, feats:])

    partial = jnp.concatenate([dot(item_cache, u, ((1,), (1,))) for u in users], axis=1)
    share = 2 * half // N_T
    partial = partial.reshape(rows, N_T, share).transpose(1, 0, 2)
    mixed = dot(attn_heads, out_proj, ((1,), (0,))).astype(BF16).reshape(N_T, tokens // N_T, width)
    got = lax.all_to_all(jnp.concatenate([mixed, *three_terms(partial)], axis=2), TENSOR, 0, 0)
    got = jnp.sum(got.astype(F32), axis=0)
    own_tokens = tokens // N_T
    own_residual = lax.dynamic_slice_in_dim(residual, t_index * own_tokens, own_tokens, 0)
    hidden_own = got[:, :width] + own_residual.astype(F32)
    scores_own = (
        got[:, width : width + share]
        + got[:, width + share : width + 2 * share]
        + got[:, width + 2 * share :]
    ) * LOGIT_SCALE
    back = jnp.concatenate([hidden_own.astype(BF16), *three_terms(scores_own)], axis=1)
    back = to_all(back, TENSOR, N_T)
    hidden = back[:, :, :width].reshape(tokens, width).astype(F32)
    scores = (
        back[:, :, width : width + share].astype(F32)
        + back[:, :, width + share : width + 2 * share].astype(F32)
        + back[:, :, width + 2 * share :].astype(F32)
    )
    scores = scores.transpose(1, 0, 2).reshape(rows, 2 * half)

    owner, row_in = positive // rows, positive % rows
    column = (owner % 2 != core).astype(jnp.int32) * half + (owner // 2) * rows + row_in
    maxima = jnp.max(scores, axis=1, keepdims=True)
    log_total = maxima[:, 0] + jnp.log(jnp.sum(jnp.exp(scores - maxima), axis=1))
    target = column[:, None] == lax.broadcasted_iota(jnp.int32, (1, 2 * half), 1)
    picked = jnp.sum(jnp.where(target, scores, F32(0.0)), axis=1)
    loss = jnp.sum(log_total - picked)
    grad = (jnp.exp(scores - log_total[:, None]) - target.astype(F32)).astype(BF16)
    item_grad = (
        dot(grad[:, :half], users[0], ((1,), (0,))) + dot(grad[:, half:], users[1], ((1,), (0,)))
    ) * LOGIT_SCALE

    group_rows = to_all(item_grad[:GROUP], TENSOR, N_T).transpose(1, 0, 2).reshape(GROUP, width)
    upstream = norm_gain[None, :] * (group_rows / SEQ)
    hidden = hidden.reshape(GROUP, SEQ, width)
    inverse = lax.rsqrt(jnp.mean(hidden * hidden, axis=2, keepdims=True) + NORM_EPS)
    inner = jnp.sum(upstream[:, None, :] * hidden, axis=2, keepdims=True) / width
    stream = inverse * upstream[:, None, :] - hidden * (inverse * inverse * inverse * inner)
    stream = stream.astype(BF16).reshape(tokens, width)
    head_grad = dot(stream, out_proj, ((1,), (1,))).astype(BF16)

    cut = width // (2 * N_P)
    weight = dot(stream, attn_heads, ((0,), (0,))).reshape(N_P, 2, cut, heads)
    give = lax.dynamic_index_in_dim(weight, 1 - core, 1, keepdims=False).astype(BF16)
    keep = lax.dynamic_index_in_dim(weight, core, 1, keepdims=False)
    loss_row = jnp.stack(three_terms(loss))
    loss_rows = jnp.zeros((8, heads), BF16).at[0, :3].set(loss_row)
    grad_give = grad[:, half:].reshape(-1, heads)
    packed = jnp.concatenate([give.reshape(-1, heads), grad_give, loss_rows], axis=0)
    packed = lax.ppermute(packed, "c", SWAP)
    n_w, n_g = N_P * cut, grad_give.shape[0]
    keep = (keep + packed[:n_w].reshape(N_P, cut, heads).astype(F32)).astype(BF16)
    both = jnp.stack([grad[:, :half], packed[n_w : n_w + n_g].reshape(rows, half)])
    both = both.reshape(2, rows, N_P, rows).transpose(2, 0, 1, 3)
    loss = loss + jnp.sum(packed[n_w + n_g, :3].astype(F32))
    loss_rows = jnp.zeros((8, heads), BF16).at[0, :3].set(jnp.stack(three_terms(loss)))
    tile = 2 * rows * rows // heads
    final = jnp.concatenate(
        [
            keep,
            both.reshape(N_P, tile, heads),
            jnp.broadcast_to(loss_rows[None], (N_P, 8, heads)),
        ],
        axis=1,
    )
    final = lax.all_to_all(final, PLANE, 0, 0)
    weight_grad = jnp.sum(final[:, :cut].astype(F32), axis=0).T
    loss_mean = jnp.sum(final[:, cut + tile, :3].astype(F32)) / (2 * half)
    by_user = final[:, cut : cut + tile].reshape(N_P, 2, rows, rows)
    user_grad = (
        dot(by_user[:, 0].reshape(half, rows), items[0], ((0,), (0,)))
        + dot(by_user[:, 1].reshape(half, rows), items[1], ((0,), (0,)))
    ) * LOGIT_SCALE
    return (loss_mean, item_grad, user_grad, head_grad, weight_grad)


def solution(mesh):
    names, sizes = zip(*AXES)
    fine = Mesh(mesh.devices.reshape(sizes), names)
    both = P(DP, TENSOR)
    return jax.shard_map(
        per_device,
        mesh=fine,
        in_specs=(both, both, P(DP), both, P(DP, None), P(TENSOR, None), P()),
        out_specs=(P(), both, both, both, P(TENSOR, DP)),
        check_vma=False,
    )
```

```python
import jax
import jax.numpy as jnp
from jax import lax
from jax.sharding import Mesh, PartitionSpec as P

BF16 = jnp.bfloat16
F32 = jnp.float32
LOGIT_SCALE = 50.0
NORM_EPS = 1e-06
GROUP = 8
SEQ = 32
AXES = (("zl", 4), ("y", 8), ("c", 2), ("x", 4), ("zh", 2))
TENSOR = ("x", "zh")
PLANE = ("zl", "y")
DP = ("zl", "y", "c")
N_T = 8
N_P = 32


def xor(axis, size, bits):
    return dict(axis_name=axis, perm=[(i, i ^ bits) for i in range(size)])


def swap(value):
    return lax.ppermute(value, **xor("c", 2, 1))


def three_terms(value):
    high = lax.reduce_precision(value, 8, 7)
    rest = value - high
    middle = lax.reduce_precision(rest, 8, 7)
    low = lax.reduce_precision(rest - middle, 8, 7)
    return high.astype(BF16), middle.astype(BF16), low.astype(BF16)


def to_all(value, axes, count):
    return lax.all_to_all(jnp.broadcast_to(value[None], (count,) + value.shape), axes, 0, 0)


def dot(a, b, dims):
    return lax.dot_general(a, b, (dims, ((), ())), preferred_element_type=F32)


def by_xor(value, index):
    shape = value.shape
    for bit in (1, 2, 4):
        pairs = value.reshape((N_T // (2 * bit), 2, bit) + shape[1:])
        flipped = pairs[:, ::-1].reshape(shape)
        value = jnp.where((index & bit) != 0, flipped, value)
    return value


def core_major(value):
    lead, width = value.shape[:-1], value.shape[-1]
    cut = width // (2 * N_P)
    return value.reshape(lead + (N_P, 2, cut)).swapaxes(-3, -2).reshape(lead + (width,))


def per_device(item_cache, user_cache, positive, attn_heads, residual, out_proj, norm_gain):
    rows, feats = item_cache.shape
    width = out_proj.shape[1]
    tokens, heads = attn_heads.shape
    half = N_P * rows
    core = lax.axis_index("c")
    t_index = lax.axis_index(TENSOR)
    x_block = tokens // 4
    own_tokens = tokens // N_T

    attn = by_xor(attn_heads.reshape(N_T, own_tokens, heads), t_index).reshape(tokens, heads)
    mixed = dot(attn, out_proj, ((1,), (0,))).astype(BF16)
    from_x = [
        lax.ppermute(mixed[k * x_block : (k + 1) * x_block], **xor("x", 4, k)) for k in (1, 2, 3)
    ]

    users_own = to_all(user_cache, PLANE, N_P).reshape(half, feats)
    users_own, *from_x = lax.optimization_barrier((users_own, *from_x))
    users = (users_own, swap(users_own))
    mixed_x = mixed[:x_block].astype(F32) + sum(part.astype(F32) for part in from_x)
    from_z = lax.ppermute(mixed_x[own_tokens:].astype(BF16), **xor("zh", 2, 1))

    partial = jnp.concatenate([dot(item_cache, u, ((1,), (1,))) for u in users], axis=1)
    share = 2 * half // N_T
    partial = partial.reshape(rows, N_T, share).transpose(1, 0, 2)
    scores_own = jnp.sum(lax.all_to_all(partial, TENSOR, 0, 0), axis=0) * LOGIT_SCALE
    scores_own, from_z = lax.optimization_barrier((scores_own, from_z))
    own_residual = lax.dynamic_slice_in_dim(residual, t_index * own_tokens, own_tokens, 0)
    hidden_own = mixed_x[:own_tokens] + from_z.astype(F32) + own_residual.astype(F32)
    hidden_own = core_major(hidden_own.astype(BF16))
    hidden_z = lax.ppermute(hidden_own, **xor("zh", 2, 1))
    scores = to_all(scores_own, TENSOR, N_T).transpose(1, 0, 2).reshape(rows, 2 * half)
    scores, hidden_z = lax.optimization_barrier((scores, hidden_z))
    hidden_x = jnp.concatenate([hidden_own, hidden_z], axis=0)
    hidden_x = [hidden_x] + [lax.ppermute(hidden_x, **xor("x", 4, k)) for k in (1, 2, 3)]

    owner, row_in = positive // rows, positive % rows
    column = (owner % 2 != core).astype(jnp.int32) * half + (owner // 2) * rows + row_in
    maxima = jnp.max(scores, axis=1, keepdims=True)
    log_total = maxima[:, 0] + jnp.log(jnp.sum(jnp.exp(scores - maxima), axis=1))
    target = column[:, None] == lax.broadcasted_iota(jnp.int32, (1, 2 * half), 1)
    picked = jnp.sum(jnp.where(target, scores, F32(0.0)), axis=1)
    losses = jnp.concatenate(three_terms(log_total - picked))
    grad = (jnp.exp(scores - log_total[:, None]) - target.astype(F32)).astype(BF16)
    item_grad = (
        dot(grad[:, :half], users[0], ((1,), (0,))) + dot(grad[:, half:], users[1], ((1,), (0,)))
    ) * LOGIT_SCALE

    group_rows = to_all(item_grad[:GROUP], TENSOR, N_T)
    item_cache, group_rows = lax.optimization_barrier((item_cache, group_rows))
    items_own = to_all(item_cache, PLANE, N_P).reshape(half, feats)
    group_rows = core_major(group_rows.transpose(1, 0, 2).reshape(GROUP, width))
    upstream = core_major(norm_gain)[None, :] * (by_xor(group_rows, t_index) / SEQ)
    hidden = jnp.concatenate(hidden_x, axis=0).reshape(GROUP, SEQ, width).astype(F32)
    inverse = lax.rsqrt(jnp.mean(hidden * hidden, axis=2, keepdims=True) + NORM_EPS)
    inner = jnp.sum(upstream[:, None, :] * hidden, axis=2, keepdims=True) / width
    stream = inverse * upstream[:, None, :] - hidden * (inverse * inverse * inverse * inner)
    stream = stream.astype(BF16).reshape(tokens, width)

    cut = width // (2 * N_P)
    side = width // 2
    grad_losses = jnp.zeros((8, half), BF16).at[0, : 3 * rows].set(losses)
    other = swap(jnp.concatenate([grad[:, half:], grad_losses], axis=0))
    attn_other = swap(attn)
    stream_other = swap(lax.dynamic_slice_in_dim(stream, (1 - core) * side, side, 1))
    stream_keep = lax.dynamic_slice_in_dim(stream, core * side, side, 1)
    weight = dot(stream_keep, attn, ((0,), (0,))) + dot(stream_other, attn_other, ((0,), (0,)))
    weight = weight.astype(BF16).reshape(N_P, cut, heads)
    both = jnp.stack([grad[:, :half], other[:rows]])
    both = both.reshape(2, rows, N_P, rows).transpose(2, 0, 1, 3)
    losses = jnp.concatenate([losses, other[rows, : 3 * rows]])
    losses = jnp.zeros((8, heads), BF16).at[0, : 6 * rows].set(losses)
    tile = 2 * rows * rows // heads
    final = jnp.concatenate(
        [weight, both.reshape(N_P, tile, heads), jnp.broadcast_to(losses[None], (N_P, 8, heads))],
        axis=1,
    )
    final = lax.all_to_all(final, PLANE, 0, 0)
    out_proj = core_major(out_proj)
    head_grad = dot(stream, out_proj, ((1,), (1,))).astype(BF16)
    head_grad = by_xor(head_grad.reshape(N_T, own_tokens, heads), t_index).reshape(tokens, heads)
    weight_grad = jnp.sum(final[:, :cut].astype(F32), axis=0).T
    loss_mean = jnp.sum(final[:, cut + tile].astype(F32)) / (2 * half)
    by_user = final[:, cut : cut + tile].reshape(N_P, 2, rows, rows)
    items = (items_own, swap(items_own))
    user_grad = (
        dot(by_user[:, 0].reshape(half, rows), items[0], ((0,), (0,)))
        + dot(by_user[:, 1].reshape(half, rows), items[1], ((0,), (0,)))
    ) * LOGIT_SCALE
    return (loss_mean, item_grad, user_grad, head_grad, weight_grad)


def solution(mesh):
    names, sizes = zip(*AXES)
    fine = Mesh(mesh.devices.reshape(sizes), names)
    both = P(DP, TENSOR)
    return jax.shard_map(
        per_device,
        mesh=fine,
        in_specs=(both, both, P(DP), both, P(DP, None), P(TENSOR, None), P()),
        out_specs=(P(), both, both, both, P(TENSOR, DP)),
        check_vma=False,
    )
```

```python
import jax
import jax.numpy as jnp
from jax import lax
from jax.sharding import Mesh, PartitionSpec as P

BF16 = jnp.bfloat16
F32 = jnp.float32
LOGIT_SCALE = 50.0
NORM_EPS = 1e-06
GROUP = 8
SEQ = 32
AXES = (("zl", 4), ("y", 8), ("c", 2), ("x", 4), ("zh", 2))
TENSOR = ("x", "zh")
PLANE = ("zl", "y")
DP = ("zl", "y", "c")
N_T = 8
N_P = 32


def xor(axis, size, bits):
    return dict(axis_name=axis, perm=[(i, i ^ bits) for i in range(size)])


def swap(value):
    return lax.ppermute(value, **xor("c", 2, 1))


def three_terms(value):
    high = lax.reduce_precision(value, 8, 7)
    rest = value - high
    middle = lax.reduce_precision(rest, 8, 7)
    low = lax.reduce_precision(rest - middle, 8, 7)
    return high.astype(BF16), middle.astype(BF16), low.astype(BF16)


def to_all(value, axes, count):
    return lax.all_to_all(jnp.broadcast_to(value[None], (count,) + value.shape), axes, 0, 0)


def dot(a, b, dims):
    return lax.dot_general(a, b, (dims, ((), ())), preferred_element_type=F32)


def by_xor(value, index):
    parts = [lax.dynamic_slice_in_dim(value, r ^ index, 1, 0) for r in range(value.shape[0])]
    return jnp.concatenate(parts, axis=0)


def core_major(value):
    lead, width = value.shape[:-1], value.shape[-1]
    cut = width // (2 * N_P)
    return value.reshape(lead + (N_P, 2, cut)).swapaxes(-3, -2).reshape(lead + (width,))


def per_device(item_cache, user_cache, positive, attn_heads, residual, out_proj, norm_gain):
    rows, feats = item_cache.shape
    width = out_proj.shape[1]
    tokens, heads = attn_heads.shape
    half = N_P * rows
    core = lax.axis_index("c")
    x_block = tokens // 4

    x_index = lax.axis_index("x")
    attn = by_xor(attn_heads.reshape(4, x_block, heads), x_index).reshape(tokens, heads)
    mixed = dot(attn, out_proj, ((1,), (0,))).astype(BF16)
    from_x = [
        lax.ppermute(mixed[k * x_block : (k + 1) * x_block], **xor("x", 4, k)) for k in (1, 2, 3)
    ]

    mixed_x = mixed[:x_block].astype(F32) + sum(part.astype(F32) for part in from_x)
    from_z = lax.ppermute(mixed_x.astype(BF16), **xor("zh", 2, 1))
    residual_x = lax.dynamic_slice_in_dim(residual, x_index * x_block, x_block, 0)
    hidden_x = core_major((mixed_x + from_z.astype(F32) + residual_x.astype(F32)).astype(BF16))
    hidden_x = [hidden_x] + [lax.ppermute(hidden_x, **xor("x", 4, k)) for k in (1, 2, 3)]

    items = lax.all_gather(item_cache, DP, axis=0, tiled=True)
    users_own = to_all(user_cache, PLANE, N_P).reshape(half, feats)
    users = (users_own, swap(users_own))

    partial = jnp.concatenate([dot(item_cache, u, ((1,), (1,))) for u in users], axis=1)
    share = 2 * half // N_T
    partial = partial.reshape(rows, N_T, share).transpose(1, 0, 2)
    scores_own = jnp.sum(lax.all_to_all(partial, TENSOR, 0, 0), axis=0) * LOGIT_SCALE
    scores = to_all(scores_own, TENSOR, N_T).transpose(1, 0, 2).reshape(rows, 2 * half)

    owner, row_in = positive // rows, positive % rows
    column = (owner % 2 != core).astype(jnp.int32) * half + (owner // 2) * rows + row_in
    maxima = jnp.max(scores, axis=1, keepdims=True)
    log_total = maxima[:, 0] + jnp.log(jnp.sum(jnp.exp(scores - maxima), axis=1))
    target = column[:, None] == lax.broadcasted_iota(jnp.int32, (1, 2 * half), 1)
    picked = jnp.sum(jnp.where(target, scores, F32(0.0)), axis=1)
    losses = jnp.concatenate(three_terms(log_total - picked))
    grad = (jnp.exp(scores - log_total[:, None]) - target.astype(F32)).astype(BF16)
    item_grad = (
        dot(grad[:, :half], users[0], ((1,), (0,))) + dot(grad[:, half:], users[1], ((1,), (0,)))
    ) * LOGIT_SCALE

    group_rows = to_all(item_grad[:GROUP], TENSOR, N_T)
    group_rows = core_major(group_rows.transpose(1, 0, 2).reshape(GROUP, width))
    upstream = core_major(norm_gain)[None, :] * (
        by_xor(group_rows.reshape(4, -1), x_index).reshape(GROUP, width) / SEQ
    )
    hidden = jnp.concatenate(hidden_x, axis=0).reshape(GROUP, SEQ, width).astype(F32)
    inverse = lax.rsqrt(jnp.mean(hidden * hidden, axis=2, keepdims=True) + NORM_EPS)
    inner = jnp.sum(upstream[:, None, :] * hidden, axis=2, keepdims=True) / width
    stream = inverse * upstream[:, None, :] - hidden * (inverse * inverse * inverse * inner)
    stream = stream.astype(BF16).reshape(tokens, width)

    cut = width // (2 * N_P)
    side = width // 2
    grad_losses = jnp.zeros((8, half), BF16).at[0, : 3 * rows].set(losses)
    other = swap(jnp.concatenate([grad[:, half:], grad_losses], axis=0))
    attn_other = swap(attn)
    stream_other = swap(lax.dynamic_slice_in_dim(stream, (1 - core) * side, side, 1))
    stream_keep = lax.dynamic_slice_in_dim(stream, core * side, side, 1)
    weight = dot(stream_keep, attn, ((0,), (0,))) + dot(stream_other, attn_other, ((0,), (0,)))
    weight = weight.astype(BF16).reshape(N_P, cut, heads)
    both = jnp.stack([grad[:, :half], other[:rows]])
    both = jnp.where(core == 0, both, both[::-1])
    both = both.reshape(2, rows, N_P, rows).transpose(2, 0, 1, 3)
    losses = jnp.concatenate([losses, other[rows, : 3 * rows]])
    losses = jnp.zeros((8, heads), BF16).at[0, : 6 * rows].set(losses)
    tile = 2 * rows * rows // heads
    final = jnp.concatenate(
        [weight, both.reshape(N_P, tile, heads), jnp.broadcast_to(losses[None], (N_P, 8, heads))],
        axis=1,
    )
    final = lax.all_to_all(final, PLANE, 0, 0)
    out_proj = core_major(out_proj)
    head_grad = dot(stream, out_proj, ((1,), (1,))).astype(BF16)
    head_grad = by_xor(head_grad.reshape(4, x_block, heads), x_index).reshape(tokens, heads)
    weight_grad = jnp.sum(final[:, :cut].astype(F32), axis=0).T
    loss_mean = jnp.sum(final[:, cut + tile].astype(F32)) / (2 * half)
    by_user = final[:, cut : cut + tile].reshape(2 * half, rows)
    user_grad = dot(by_user, items, ((0,), (0,))) * LOGIT_SCALE
    return (loss_mean, item_grad, user_grad, head_grad, weight_grad)


def solution(mesh):
    names, sizes = zip(*AXES)
    fine = Mesh(mesh.devices.reshape(sizes), names)
    both = P(DP, TENSOR)
    return jax.shard_map(
        per_device,
        mesh=fine,
        in_specs=(both, both, P(DP), both, P(DP, None), P(TENSOR, None), P()),
        out_specs=(P(), both, both, both, P(TENSOR, DP)),
        check_vma=False,
    )
```

```python
import jax
import jax.numpy as jnp
from jax import lax
from jax.sharding import Mesh, PartitionSpec as P

BF16 = jnp.bfloat16
F32 = jnp.float32
LOGIT_SCALE = 50.0
NORM_EPS = 1e-06
GROUP = 8
SEQ = 32
AXES = (("zl", 4), ("y", 8), ("c", 2), ("x", 4), ("zh", 2))
TENSOR = ("x", "zh")
PLANE = ("zl", "y")
DP = ("zl", "y", "c")
N_T = 8
N_P = 32


def xor(axis, size, bits):
    return dict(axis_name=axis, perm=[(i, i ^ bits) for i in range(size)])


def swap(value):
    return lax.ppermute(value, **xor("c", 2, 1))


def three_terms(value):
    high = lax.reduce_precision(value, 8, 7)
    rest = value - high
    middle = lax.reduce_precision(rest, 8, 7)
    low = lax.reduce_precision(rest - middle, 8, 7)
    return high.astype(BF16), middle.astype(BF16), low.astype(BF16)


def to_all(value, axes, count):
    return lax.all_to_all(jnp.broadcast_to(value[None], (count,) + value.shape), axes, 0, 0)


def dot(a, b, dims):
    return lax.dot_general(a, b, (dims, ((), ())), preferred_element_type=F32)


def by_xor(value, index):
    parts = [lax.dynamic_slice_in_dim(value, r ^ index, 1, 0) for r in range(value.shape[0])]
    return jnp.concatenate(parts, axis=0)


def core_major(value):
    lead, width = value.shape[:-1], value.shape[-1]
    cut = width // (2 * N_P)
    return value.reshape(lead + (N_P, 2, cut)).swapaxes(-3, -2).reshape(lead + (width,))


def after(value, *others):
    return lax.optimization_barrier((value, *others))[0]


def per_device(item_cache, user_cache, positive, attn_heads, residual, out_proj, norm_gain):
    rows, feats = item_cache.shape
    width = out_proj.shape[1]
    tokens, heads = attn_heads.shape
    half = N_P * rows
    core = lax.axis_index("c")
    x_index = lax.axis_index("x")
    z_index = lax.axis_index("zh")
    x_block = tokens // 4
    z_block = x_block // 2

    attn = by_xor(attn_heads.reshape(4, x_block, heads), x_index).reshape(tokens, heads)
    attn_other = swap(attn)
    mixed = dot(attn, out_proj, ((1,), (0,))).astype(BF16)
    from_x = [
        lax.ppermute(mixed[k * x_block : (k + 1) * x_block], **xor("x", 4, k)) for k in (1, 2, 3)
    ]
    mixed_x = mixed[:x_block].astype(F32) + sum(part.astype(F32) for part in from_x)
    mixed_x = mixed_x.reshape(2, z_block, width)
    mixed_give = lax.dynamic_index_in_dim(mixed_x, 1 - z_index, 0, keepdims=False)
    mixed_keep = lax.dynamic_index_in_dim(mixed_x, z_index, 0, keepdims=False)
    from_z = lax.ppermute(mixed_give.astype(BF16), **xor("zh", 2, 1))

    users_own = to_all(user_cache, PLANE, N_P).reshape(half, feats)
    users = (users_own, swap(users_own))

    partial = jnp.concatenate([dot(item_cache, u, ((1,), (1,))) for u in users], axis=1)
    share = 2 * half // N_T
    partial = partial.reshape(rows, N_T, share).transpose(1, 0, 2)
    scores_own = jnp.sum(lax.all_to_all(partial, TENSOR, 0, 0), axis=0) * LOGIT_SCALE
    scores = to_all(scores_own, TENSOR, N_T).transpose(1, 0, 2).reshape(rows, 2 * half)

    own_tokens = (2 * x_index + z_index) * z_block
    own_residual = lax.dynamic_slice_in_dim(residual, own_tokens, z_block, 0).astype(F32)
    hidden_own = mixed_keep + after(from_z, partial).astype(F32) + own_residual
    hidden_own = core_major(hidden_own.astype(BF16))
    hidden_z = after(lax.ppermute(hidden_own, **xor("zh", 2, 1)), scores_own)
    pair = jnp.stack([hidden_own, hidden_z])
    hidden_x = jnp.where(z_index == 0, pair, pair[::-1]).reshape(x_block, width)
    hidden_x = [hidden_x] + [lax.ppermute(hidden_x, **xor("x", 4, k)) for k in (1, 2, 3)]

    owner, row_in = positive // rows, positive % rows
    column = (owner % 2 != core).astype(jnp.int32) * half + (owner // 2) * rows + row_in
    maxima = jnp.max(scores, axis=1, keepdims=True)
    log_total = maxima[:, 0] + jnp.log(jnp.sum(jnp.exp(scores - maxima), axis=1))
    target = column[:, None] == lax.broadcasted_iota(jnp.int32, (1, 2 * half), 1)
    picked = jnp.sum(jnp.where(target, scores, F32(0.0)), axis=1)
    losses = jnp.concatenate(three_terms(log_total - picked))
    grad = (jnp.exp(scores - log_total[:, None]) - target.astype(F32)).astype(BF16)
    item_grad = (
        dot(grad[:, :half], users[0], ((1,), (0,))) + dot(grad[:, half:], users[1], ((1,), (0,)))
    ) * LOGIT_SCALE
    group_rows = to_all(item_grad[:GROUP], TENSOR, N_T)

    grad_losses = jnp.zeros((8, half), BF16).at[0, : 3 * rows].set(losses)
    other = swap(jnp.concatenate([grad[:, half:], grad_losses], axis=0))
    losses = jnp.concatenate([losses, other[rows, : 3 * rows]])
    losses = jnp.zeros((8, heads), BF16).at[0, : 6 * rows].set(losses)
    both = jnp.concatenate([grad[:, :half], other[:rows]], axis=0)
    both = both.T.reshape(N_P, rows, 2 * rows)
    by_plane = jnp.concatenate(
        [jnp.broadcast_to(item_cache[None], (N_P, rows, feats)), both], axis=2
    )
    group_rows = after(group_rows, by_plane, losses)
    by_plane = lax.all_to_all(after(by_plane, group_rows), PLANE, 0, 0)

    group_rows = core_major(group_rows.transpose(1, 0, 2).reshape(GROUP, width))
    upstream = core_major(norm_gain)[None, :] * (
        by_xor(group_rows.reshape(4, -1), x_index).reshape(GROUP, width) / SEQ
    )
    hidden = jnp.concatenate(hidden_x, axis=0).reshape(GROUP, SEQ, width).astype(F32)
    inverse = lax.rsqrt(jnp.mean(hidden * hidden, axis=2, keepdims=True) + NORM_EPS)
    inner = jnp.sum(upstream[:, None, :] * hidden, axis=2, keepdims=True) / width
    stream = inverse * upstream[:, None, :] - hidden * (inverse * inverse * inverse * inner)
    stream = stream.astype(BF16).reshape(tokens, width)

    cut = width // (2 * N_P)
    side = width // 2
    stream_other = swap(lax.dynamic_slice_in_dim(stream, (1 - core) * side, side, 1))
    stream_keep = lax.dynamic_slice_in_dim(stream, core * side, side, 1)
    weight = dot(stream_keep, attn, ((0,), (0,))) + dot(stream_other, attn_other, ((0,), (0,)))
    weight = weight.astype(BF16).reshape(N_P, cut, heads)
    weight, by_plane = lax.optimization_barrier((weight, by_plane))
    final = jnp.concatenate([weight, jnp.broadcast_to(losses[None], (N_P, 8, heads))], axis=1)
    final = lax.all_to_all(final, PLANE, 0, 0)
    out_proj = core_major(out_proj)
    head_grad = dot(stream, out_proj, ((1,), (1,))).astype(BF16)
    head_grad = by_xor(head_grad.reshape(4, x_block, heads), x_index).reshape(tokens, heads)
    items_own = by_plane[:, :, :feats].reshape(half, feats)
    by_item = by_plane[:, :, feats:].reshape(N_P, rows, 2, rows).transpose(2, 0, 3, 1)
    by_item = by_item.reshape(2, half, rows)
    user_grad = (
        dot(by_item[0], items_own, ((0,), (0,))) + dot(by_item[1], swap(items_own), ((0,), (0,)))
    ) * LOGIT_SCALE
    weight_grad = jnp.sum(final[:, :cut].astype(F32), axis=0).T
    loss_mean = jnp.sum(final[:, cut].astype(F32)) / (2 * half)
    return (loss_mean, item_grad, user_grad, head_grad, weight_grad)


def solution(mesh):
    names, sizes = zip(*AXES)
    fine = Mesh(mesh.devices.reshape(sizes), names)
    both = P(DP, TENSOR)
    return jax.shard_map(
        per_device,
        mesh=fine,
        in_specs=(both, both, P(DP), both, P(DP, None), P(TENSOR, None), P()),
        out_specs=(P(), both, both, both, P(TENSOR, DP)),
        check_vma=False,
    )
```

```python
import jax
import jax.numpy as jnp
from jax import lax
from jax.sharding import Mesh, PartitionSpec as P

BF16 = jnp.bfloat16
F32 = jnp.float32
LOGIT_SCALE = 50.0
NORM_EPS = 1e-06
GROUP = 8
SEQ = 32
AXES = (("zl", 4), ("y", 8), ("c", 2), ("x", 4), ("zh", 2))
TENSOR = ("x", "zh")
PLANE = ("zl", "y")
DP = ("zl", "y", "c")
N_T = 8
N_P = 32


def xor(axis, size, bits):
    return dict(axis_name=axis, perm=[(i, i ^ bits) for i in range(size)])


def swap(value):
    return lax.ppermute(value, **xor("c", 2, 1))


def three_terms(value):
    high = lax.reduce_precision(value, 8, 7)
    rest = value - high
    middle = lax.reduce_precision(rest, 8, 7)
    low = lax.reduce_precision(rest - middle, 8, 7)
    return high.astype(BF16), middle.astype(BF16), low.astype(BF16)


def to_all(value, axes, count):
    return lax.all_to_all(jnp.broadcast_to(value[None], (count,) + value.shape), axes, 0, 0)


def dot(a, b, dims):
    return lax.dot_general(a, b, (dims, ((), ())), preferred_element_type=F32)


def by_xor(value, index):
    parts = [lax.dynamic_slice_in_dim(value, r ^ index, 1, 0) for r in range(value.shape[0])]
    return jnp.concatenate(parts, axis=0)


def core_major(value):
    lead, width = value.shape[:-1], value.shape[-1]
    cut = width // (2 * N_P)
    return value.reshape(lead + (N_P, 2, cut)).swapaxes(-3, -2).reshape(lead + (width,))


def tie(value, other):
    corner = other.reshape(-1, other.shape[-1])[:1, :1].reshape((1,) * value.ndim)
    return value + (corner * 0).astype(value.dtype)


def per_device(item_cache, user_cache, positive, attn_heads, residual, out_proj, norm_gain):
    rows, feats = item_cache.shape
    width = out_proj.shape[1]
    tokens, heads = attn_heads.shape
    half = N_P * rows
    core = lax.axis_index("c")
    x_index = lax.axis_index("x")
    z_index = lax.axis_index("zh")
    x_block = tokens // 4
    z_block = x_block // 2

    attn = by_xor(attn_heads.reshape(4, x_block, heads), x_index).reshape(tokens, heads)
    mixed = dot(attn, out_proj, ((1,), (0,))).astype(BF16)
    mixed = mixed.reshape(4, 2, z_block, width)
    toward = [
        lax.ppermute(mixed[2, 0], **xor("x", 4, 1)),
        lax.ppermute(mixed[2, 1], **xor("x", 4, 3)),
    ]
    toward = [part.astype(F32) for part in toward]
    mixed_3 = jnp.stack([mixed[3, 0].astype(F32) + toward[0], mixed[3, 1].astype(F32)])
    mixed_1 = jnp.stack([mixed[1, 0].astype(F32), mixed[1, 1].astype(F32) + toward[1]])
    from_x = [
        lax.ppermute(mixed_1.astype(BF16), **xor("x", 4, 1)),
        lax.ppermute(mixed_3.astype(BF16), **xor("x", 4, 3)),
    ]
    mixed_x = mixed[0].astype(F32) + sum(part.astype(F32) for part in from_x)
    mixed_give = lax.dynamic_index_in_dim(mixed_x, 1 - z_index, 0, keepdims=False)
    mixed_keep = lax.dynamic_index_in_dim(mixed_x, z_index, 0, keepdims=False)
    mixed_give = mixed_give.astype(BF16)
    from_z = lax.ppermute(mixed_give, **xor("zh", 2, 1))

    users_own = to_all(tie(user_cache, mixed), PLANE, N_P).reshape(half, feats)
    users = (users_own, swap(users_own))

    partial = jnp.concatenate([dot(item_cache, u, ((1,), (1,))) for u in users], axis=1)
    share = 2 * half // N_T
    attn_other = swap(tie(attn, partial))
    partial = partial.reshape(rows, N_T, share).transpose(1, 0, 2)
    scores_own = jnp.sum(lax.all_to_all(partial, TENSOR, 0, 0), axis=0) * LOGIT_SCALE
    scores = to_all(scores_own, TENSOR, N_T).transpose(1, 0, 2).reshape(rows, 2 * half)

    own_tokens = (2 * x_index + z_index) * z_block
    own_residual = lax.dynamic_slice_in_dim(residual, own_tokens, z_block, 0).astype(F32)
    hidden_own = mixed_keep + tie(from_z, partial).astype(F32) + own_residual
    hidden_own = core_major(hidden_own.astype(BF16))
    hidden_z = tie(lax.ppermute(hidden_own, **xor("zh", 2, 1)), scores_own)
    pair = jnp.stack([hidden_own, hidden_z])
    hidden_0 = jnp.where(z_index == 0, pair, pair[::-1])
    hidden_1 = lax.ppermute(hidden_0, **xor("x", 4, 1))
    hidden_3 = lax.ppermute(hidden_0, **xor("x", 4, 3))
    owner, row_in = positive // rows, positive % rows
    column = (owner % 2 != core).astype(jnp.int32) * half + (owner // 2) * rows + row_in
    maxima = jnp.max(scores, axis=1, keepdims=True)
    log_total = maxima[:, 0] + jnp.log(jnp.sum(jnp.exp(scores - maxima), axis=1))
    target = column[:, None] == lax.broadcasted_iota(jnp.int32, (1, 2 * half), 1)
    picked = jnp.sum(jnp.where(target, scores, F32(0.0)), axis=1)
    losses = jnp.concatenate(three_terms(log_total - picked))
    grad = (jnp.exp(scores - log_total[:, None]) - target.astype(F32)).astype(BF16)
    item_grad = (
        dot(grad[:, :half], users[0], ((1,), (0,))) + dot(grad[:, half:], users[1], ((1,), (0,)))
    ) * LOGIT_SCALE
    group_rows = to_all(item_grad[:GROUP], TENSOR, N_T)
    hidden_2 = [
        lax.ppermute(tie(hidden_1[0], item_grad), **xor("x", 4, 3)),
        lax.ppermute(tie(hidden_3[1], item_grad), **xor("x", 4, 1)),
    ]

    grad_losses = jnp.zeros((8, half), BF16).at[0, : 3 * rows].set(losses)
    other = swap(jnp.concatenate([grad[:, half:], grad_losses], axis=0))
    losses = jnp.concatenate([losses, other[rows, : 3 * rows]])
    losses = jnp.zeros((8, heads), BF16).at[0, : 6 * rows].set(losses)
    both = jnp.concatenate([grad[:, :half], other[:rows]], axis=0)
    both = both.T.reshape(N_P, rows, 2 * rows)
    by_plane = jnp.concatenate(
        [jnp.broadcast_to(item_cache[None], (N_P, rows, feats)), both], axis=2
    )
    by_plane = lax.all_to_all(by_plane, PLANE, 0, 0)

    group_rows = core_major(group_rows.transpose(1, 0, 2).reshape(GROUP, width))
    upstream = core_major(norm_gain)[None, :] * (
        by_xor(group_rows.reshape(4, -1), x_index).reshape(GROUP, width) / SEQ
    )
    hidden_2 = tie(jnp.stack(hidden_2), group_rows)
    hidden = jnp.concatenate([hidden_0, hidden_1, hidden_2, hidden_3], axis=0).astype(F32)
    inverse = lax.rsqrt(jnp.mean(hidden * hidden, axis=2, keepdims=True) + NORM_EPS)
    inner = jnp.sum(upstream[:, None, :] * hidden, axis=2, keepdims=True) / width
    stream = inverse * upstream[:, None, :] - hidden * (inverse * inverse * inverse * inner)
    stream = stream.astype(BF16).reshape(tokens, width)

    cut = width // (2 * N_P)
    side = width // 2
    stream_other = swap(lax.dynamic_slice_in_dim(stream, (1 - core) * side, side, 1))
    stream_keep = lax.dynamic_slice_in_dim(stream, core * side, side, 1)
    attn_other = tie(attn_other, scores)
    weight = dot(stream_keep, attn, ((0,), (0,))) + dot(stream_other, attn_other, ((0,), (0,)))
    weight = weight.astype(BF16).reshape(N_P, cut, heads)
    final = jnp.concatenate([weight, jnp.broadcast_to(losses[None], (N_P, 8, heads))], axis=1)
    final = lax.all_to_all(final, PLANE, 0, 0)
    head_grad = dot(stream, core_major(tie(out_proj, weight[0])), ((1,), (1,))).astype(BF16)
    head_grad = by_xor(head_grad.reshape(4, x_block, heads), x_index).reshape(tokens, heads)
    items_own = by_plane[:, :, :feats].reshape(half, feats)
    by_item = by_plane[:, :, feats:].reshape(N_P, rows, 2, rows).transpose(2, 0, 3, 1)
    by_item = by_item.reshape(2, half, rows)
    user_grad = (
        dot(by_item[0], items_own, ((0,), (0,))) + dot(by_item[1], swap(items_own), ((0,), (0,)))
    ) * LOGIT_SCALE
    weight_grad = jnp.sum(final[:, :cut].astype(F32), axis=0).T
    loss_mean = jnp.sum(final[:, cut].astype(F32)) / (2 * half)
    return (loss_mean, item_grad, user_grad, head_grad, weight_grad)


def solution(mesh):
    names, sizes = zip(*AXES)
    fine = Mesh(mesh.devices.reshape(sizes), names)
    both = P(DP, TENSOR)
    return jax.shard_map(
        per_device,
        mesh=fine,
        in_specs=(both, both, P(DP), both, P(DP, None), P(TENSOR, None), P()),
        out_specs=(P(), both, both, both, P(TENSOR, DP)),
        check_vma=False,
    )
```

```python
import jax
import jax.numpy as jnp
from jax import lax
from jax.sharding import Mesh, PartitionSpec as P

BF16 = jnp.bfloat16
F32 = jnp.float32
LOGIT_SCALE = 50.0
NORM_EPS = 1e-06
GROUP = 8
SEQ = 32
AXES = (("zl", 4), ("y", 8), ("c", 2), ("x", 4), ("zh", 2))
TENSOR = ("x", "zh")
PLANE = ("zl", "y")
DP = ("zl", "y", "c")
N_T, N_Y, N_Z = 8, 8, 4
N_P = N_Y * N_Z


def xor(axis, size, bits):
    return dict(axis_name=axis, perm=[(i, i ^ bits) for i in range(size)])


def swap(value):
    return lax.ppermute(value, **xor("c", 2, 1))


def three_terms(value):
    high = lax.reduce_precision(value, 8, 7)
    rest = value - high
    middle = lax.reduce_precision(rest, 8, 7)
    low = lax.reduce_precision(rest - middle, 8, 7)
    return high.astype(BF16), middle.astype(BF16), low.astype(BF16)


def to_all(value, axes, count):
    return lax.all_to_all(jnp.broadcast_to(value[None], (count,) + value.shape), axes, 0, 0)


def dot(a, b, dims):
    return lax.dot_general(a, b, (dims, ((), ())), preferred_element_type=F32)


def by_xor(value, index):
    parts = [lax.dynamic_slice_in_dim(value, r ^ index, 1, 0) for r in range(value.shape[0])]
    return jnp.concatenate(parts, axis=0)


def core_major(value):
    lead, width = value.shape[:-1], value.shape[-1]
    cut = width // (2 * N_P)
    return value.reshape(lead + (N_P, 2, cut)).swapaxes(-3, -2).reshape(lead + (width,))


def tie(value, other):
    corner = other.reshape(-1, other.shape[-1])[:1, :1].reshape((1,) * value.ndim)
    return value + (corner * 0).astype(value.dtype)


def per_device(item_cache, user_cache, positive, attn_heads, residual, out_proj, norm_gain):
    rows, feats = item_cache.shape
    width = out_proj.shape[1]
    tokens, heads = attn_heads.shape
    core = lax.axis_index("c")
    x_index = lax.axis_index("x")
    z_index = lax.axis_index("zh")
    x_block = tokens // 4
    z_block = x_block // 2

    attn = by_xor(attn_heads.reshape(4, x_block, heads), x_index).reshape(tokens, heads)
    mixed = dot(attn, out_proj, ((1,), (0,))).astype(BF16)
    mixed = mixed.reshape(4, 2, z_block, width)
    toward = [
        lax.ppermute(mixed[2, 0], **xor("x", 4, 1)),
        lax.ppermute(mixed[2, 1], **xor("x", 4, 3)),
    ]
    toward = [part.astype(F32) for part in toward]
    mixed_3 = jnp.stack([mixed[3, 0].astype(F32) + toward[0], mixed[3, 1].astype(F32)])
    mixed_1 = jnp.stack([mixed[1, 0].astype(F32), mixed[1, 1].astype(F32) + toward[1]])
    from_x = [
        lax.ppermute(mixed_1.astype(BF16), **xor("x", 4, 1)),
        lax.ppermute(mixed_3.astype(BF16), **xor("x", 4, 3)),
    ]
    mixed_x = mixed[0].astype(F32) + sum(part.astype(F32) for part in from_x)
    mixed_give = lax.dynamic_index_in_dim(mixed_x, 1 - z_index, 0, keepdims=False)
    mixed_keep = lax.dynamic_index_in_dim(mixed_x, z_index, 0, keepdims=False)
    mixed_give = mixed_give.astype(BF16)

    users_own = to_all(tie(user_cache, mixed[0, 0]), "y", N_Y).reshape(N_Y * rows, feats)
    users = (users_own, swap(users_own))
    place = lax.broadcasted_iota(jnp.int32, (rows, 64), 1)
    place = jnp.where(place == 0, positive[:, None] // 64, positive[:, None] % 64).astype(BF16)
    items = jnp.concatenate([item_cache, place], axis=1)
    items = to_all(tie(items, users_own), "zl", N_Z).reshape(N_Z * rows, feats + 64)
    place = items[:, feats : feats + 2].astype(jnp.int32)
    items = items[:, :feats]
    columns = 2 * N_Y * rows
    own = N_Z * rows // N_T

    partial = jnp.concatenate([dot(items, u, ((1,), (1,))) for u in users], axis=1)
    partial = partial.reshape(N_T, own, columns)
    scores = jnp.sum(lax.all_to_all(partial, TENSOR, 0, 0), axis=0) * LOGIT_SCALE

    place = lax.dynamic_slice_in_dim(place, (2 * x_index + z_index) * own, own, 0)
    place = place[:, :1] * 64 + place[:, 1:]
    owner, row_in = place // rows, place % rows
    column = (owner % 2 != core).astype(jnp.int32) * N_Y * rows + (owner // 2 % N_Y) * rows + row_in
    column = jnp.where(owner // (2 * N_Y) == lax.axis_index("zl"), column, -1)
    target = column == lax.broadcasted_iota(jnp.int32, (1, columns), 1)
    maxima = jnp.max(scores, axis=1, keepdims=True)
    sums = jnp.sum(jnp.exp(scores - maxima), axis=1, keepdims=True)
    picked = jnp.sum(jnp.where(target, scores, F32(0.0)), axis=1, keepdims=True)
    lane = lax.broadcasted_iota(jnp.int32, (own, 128), 1)
    stats = jnp.where(lane == 0, maxima, jnp.where(lane == 1, sums, picked))
    stats = to_all(stats, "zl", N_Z)
    top = jnp.max(stats[:, :, :1], axis=0)
    log_total = top + jnp.log(jnp.sum(stats[:, :, 1:2] * jnp.exp(stats[:, :, :1] - top), axis=0))
    losses = log_total - jnp.sum(stats[:, :, 2:3], axis=0)
    grad = (jnp.exp(scores - log_total) - target.astype(F32)).astype(BF16)
    high, middle, low = three_terms(losses)
    losses = jnp.where(lane == 0, high, jnp.where(lane == 1, middle, low))
    losses = jnp.where(lane < 3, losses, BF16(0.0))
    tile = to_all(jnp.concatenate([grad, losses], axis=1), TENSOR, N_T)
    tile = tile.reshape(N_Z * rows, columns + 128)
    losses = jnp.sum(tile[:, columns:].astype(F32), axis=0, keepdims=True)
    tile = tile[:, :columns]
    item_part = dot(tile[:, : columns // 2], users[0], ((1,), (0,)))
    item_part += dot(tile[:, columns // 2 :], users[1], ((1,), (0,)))
    item_part = lax.all_to_all(item_part.reshape(N_Z, rows, feats), "zl", 0, 0)
    item_grad = jnp.sum(item_part, axis=0) * LOGIT_SCALE
    group_rows = to_all(item_grad[:GROUP], TENSOR, N_T)

    user_part = dot(tile, items, ((0,), (0,)))
    losses = jnp.pad(jnp.concatenate(three_terms(losses)), ((0, 13), (0, feats - 128)))
    give = jnp.concatenate([user_part[columns // 2 :].astype(BF16), losses], axis=0)
    give = swap(tie(give, item_part))
    losses = losses[:8].astype(F32) + give[columns // 2 : columns // 2 + 8].astype(F32)
    user_part = (user_part[: columns // 2] + give[: columns // 2].astype(F32)).astype(BF16)
    user_part = tie(user_part.reshape(N_Y, rows, feats), group_rows)
    user_grad = jnp.sum(lax.all_to_all(user_part, "y", 0, 0).astype(F32), axis=0) * LOGIT_SCALE

    from_z = lax.ppermute(mixed_give, **xor("zh", 2, 1))
    own_tokens = (2 * x_index + z_index) * z_block
    own_residual = lax.dynamic_slice_in_dim(residual, own_tokens, z_block, 0).astype(F32)
    hidden_own = mixed_keep + tie(from_z, partial).astype(F32) + own_residual
    hidden_own = core_major(hidden_own.astype(BF16))
    hidden_z = tie(lax.ppermute(hidden_own, **xor("zh", 2, 1)), scores)
    pair = jnp.stack([hidden_own, hidden_z])
    hidden_0 = jnp.where(z_index == 0, pair, pair[::-1])
    hidden_1 = lax.ppermute(hidden_0, **xor("x", 4, 1))
    hidden_3 = lax.ppermute(hidden_0, **xor("x", 4, 3))
    hidden_2 = [
        lax.ppermute(tie(hidden_1[0], grad), **xor("x", 4, 3)),
        lax.ppermute(tie(hidden_3[1], grad), **xor("x", 4, 1)),
    ]
    attn_other = swap(tie(attn, partial))

    group_rows = core_major(group_rows.transpose(1, 0, 2).reshape(GROUP, width))
    upstream = core_major(norm_gain)[None, :] * (
        by_xor(group_rows.reshape(4, -1), x_index).reshape(GROUP, width) / SEQ
    )
    hidden_2 = tie(jnp.stack(hidden_2), item_grad)
    hidden = jnp.concatenate([hidden_0, hidden_1, hidden_2, hidden_3], axis=0).astype(F32)
    inverse = lax.rsqrt(jnp.mean(hidden * hidden, axis=2, keepdims=True) + NORM_EPS)
    inner = jnp.sum(upstream[:, None, :] * hidden, axis=2, keepdims=True) / width
    stream = inverse * upstream[:, None, :] - hidden * (inverse * inverse * inverse * inner)
    stream = stream.astype(BF16).reshape(tokens, width)

    cut = width // (2 * N_P)
    side = width // 2
    stream_other = swap(lax.dynamic_slice_in_dim(stream, (1 - core) * side, side, 1))
    stream_keep = lax.dynamic_slice_in_dim(stream, core * side, side, 1)
    attn_other = tie(attn_other, scores)
    weight = dot(stream_keep, attn, ((0,), (0,))) + dot(stream_other, attn_other, ((0,), (0,)))
    weight = weight.astype(BF16).reshape(N_P, cut, heads)
    losses = losses[:1, :heads] + losses[1:2, :heads] + losses[2:3, :heads]
    losses = jnp.pad(jnp.concatenate(three_terms(losses)), ((0, 5), (0, 0)))
    final = jnp.concatenate([weight, jnp.broadcast_to(losses[None], (N_P, 8, heads))], axis=1)
    final = lax.all_to_all(final, PLANE, 0, 0)
    head_grad = dot(stream, core_major(tie(out_proj, weight[0])), ((1,), (1,))).astype(BF16)
    head_grad = by_xor(head_grad.reshape(4, x_block, heads), x_index).reshape(tokens, heads)
    weight_grad = jnp.sum(final[:, :cut].astype(F32), axis=0).T
    loss_mean = jnp.sum(final[:, cut].astype(F32)) / (N_Z * 2 * N_P * rows)
    loss_mean += jnp.sum(final[:, cut + 1 : cut + 3].astype(F32)) / (N_Z * 2 * N_P * rows)
    return (loss_mean, item_grad, user_grad, head_grad, weight_grad)


def solution(mesh):
    names, sizes = zip(*AXES)
    fine = Mesh(mesh.devices.reshape(sizes), names)
    both = P(DP, TENSOR)
    return jax.shard_map(
        per_device,
        mesh=fine,
        in_specs=(both, both, P(DP), both, P(DP, None), P(TENSOR, None), P()),
        out_specs=(P(), both, both, both, P(TENSOR, DP)),
        check_vma=False,
    )
```

```python
import jax
import jax.numpy as jnp
from jax import lax
from jax.sharding import Mesh, PartitionSpec as P

BF16 = jnp.bfloat16
F32 = jnp.float32
LOGIT_SCALE = 50.0
NORM_EPS = 1e-06
GROUP = 8
SEQ = 32
AXES = (("zl", 4), ("y", 8), ("c", 2), ("x", 4), ("zh", 2))
TENSOR = ("x", "zh")
PLANE = ("zl", "y")
DP = ("zl", "y", "c")
N_T = 8
N_P = 32


def xor(axis, size, bits):
    return dict(axis_name=axis, perm=[(i, i ^ bits) for i in range(size)])


def swap(value):
    return lax.ppermute(value, **xor("c", 2, 1))


def three_terms(value):
    high = lax.reduce_precision(value, 8, 7)
    rest = value - high
    middle = lax.reduce_precision(rest, 8, 7)
    low = lax.reduce_precision(rest - middle, 8, 7)
    return high.astype(BF16), middle.astype(BF16), low.astype(BF16)


def to_all(value, axes, count):
    return lax.all_to_all(jnp.broadcast_to(value[None], (count,) + value.shape), axes, 0, 0)


def dot(a, b, dims):
    return lax.dot_general(a, b, (dims, ((), ())), preferred_element_type=F32)


def by_xor(value, index):
    parts = [lax.dynamic_slice_in_dim(value, r ^ index, 1, 0) for r in range(value.shape[0])]
    return jnp.concatenate(parts, axis=0)


def core_major(value):
    lead, width = value.shape[:-1], value.shape[-1]
    cut = width // (2 * N_P)
    return value.reshape(lead + (N_P, 2, cut)).swapaxes(-3, -2).reshape(lead + (width,))


def tie(value, column):
    return value + (column * 0).astype(value.dtype)


def per_device(item_cache, user_cache, positive, attn_heads, residual, out_proj, norm_gain):
    rows, feats = item_cache.shape
    width = out_proj.shape[1]
    tokens, heads = attn_heads.shape
    half = N_P * rows
    core = lax.axis_index("c")
    x_index = lax.axis_index("x")
    z_index = lax.axis_index("zh")
    x_block = tokens // 4
    z_block = x_block // 2

    attn = by_xor(attn_heads.reshape(4, x_block, heads), x_index).reshape(tokens, heads)
    out_proj = core_major(out_proj)
    mixed = dot(attn, out_proj, ((1,), (0,))).astype(BF16)
    attn_other = swap(tie(attn, mixed[:1, :1]))
    from_x = [
        lax.ppermute(mixed[k * x_block : (k + 1) * x_block], **xor("x", 4, k)) for k in (1, 2, 3)
    ]

    users_own = to_all(user_cache, PLANE, N_P).reshape(half, feats)
    users = (users_own, swap(users_own))

    partial = jnp.concatenate([dot(item_cache, u, ((1,), (1,))) for u in users], axis=1)
    share = 2 * half // N_T
    partial = partial.reshape(rows, N_T, share).transpose(1, 0, 2)
    scores_own = jnp.sum(lax.all_to_all(partial, TENSOR, 0, 0), axis=0) * LOGIT_SCALE
    scores = to_all(scores_own, TENSOR, N_T).transpose(1, 0, 2).reshape(rows, 2 * half)

    mixed_x = tie(mixed[:x_block].astype(F32), partial.reshape(-1, share)[:x_block, :1])
    mixed_x = mixed_x + sum(part.astype(F32) for part in from_x)
    mixed_x = mixed_x.reshape(2, z_block, width)
    mixed_give = lax.dynamic_index_in_dim(mixed_x, 1 - z_index, 0, keepdims=False)
    mixed_keep = lax.dynamic_index_in_dim(mixed_x, z_index, 0, keepdims=False)
    own_tokens = (2 * x_index + z_index) * z_block
    own_residual = lax.dynamic_slice_in_dim(residual, own_tokens, z_block, 0)
    own_residual = lax.optimization_barrier(core_major(own_residual))
    own_residual = tie(own_residual, attn_other[:z_block, :1])
    mixed_give = tie(mixed_give, own_residual[:, :1]).astype(BF16)
    from_z = lax.ppermute(mixed_give, **xor("zh", 2, 1))
    hidden_own = mixed_keep + tie(from_z.astype(F32), scores_own[:, :1]) + own_residual.astype(F32)
    hidden_own = hidden_own.astype(BF16)

    owner, row_in = positive // rows, positive % rows
    column = (owner % 2 != core).astype(jnp.int32) * half + (owner // 2) * rows + row_in
    maxima = jnp.max(scores, axis=1, keepdims=True)
    log_total = maxima[:, 0] + jnp.log(jnp.sum(jnp.exp(scores - maxima), axis=1))
    target = column[:, None] == lax.broadcasted_iota(jnp.int32, (1, 2 * half), 1)
    picked = jnp.sum(jnp.where(target, scores, F32(0.0)), axis=1)
    losses = jnp.concatenate(three_terms(log_total - picked))
    grad = (jnp.exp(scores - log_total[:, None]) - target.astype(F32)).astype(BF16)
    item_grad = (
        dot(grad[:, :half], users[0], ((1,), (0,))) + dot(grad[:, half:], users[1], ((1,), (0,)))
    ) * LOGIT_SCALE
    group_rows = to_all(item_grad[:GROUP], TENSOR, N_T)

    grad_losses = jnp.zeros((8, half), BF16).at[0, : 3 * rows].set(losses)
    other = swap(jnp.concatenate([grad[:, half:], grad_losses], axis=0))
    hidden_z = tie(lax.ppermute(hidden_own, **xor("zh", 2, 1)), other[:rows, :1])
    pair = jnp.stack([hidden_own, hidden_z])
    hidden_0 = jnp.where(z_index == 0, pair, pair[::-1])
    hidden_1 = lax.ppermute(hidden_0, **xor("x", 4, 1))
    hidden_3 = lax.ppermute(hidden_0, **xor("x", 4, 3))
    losses = jnp.concatenate([losses, other[rows, : 3 * rows]])
    losses = jnp.zeros((8, heads), BF16).at[0, : 6 * rows].set(losses)
    both = jnp.concatenate([grad[:, :half], other[:rows]], axis=0)
    both = both.T.reshape(N_P, rows, 2 * rows)
    by_plane = jnp.concatenate(
        [jnp.broadcast_to(item_cache[None], (N_P, rows, feats)), both], axis=2
    )
    by_plane = lax.all_to_all(by_plane, PLANE, 0, 0)

    group_rows = core_major(group_rows.transpose(1, 0, 2).reshape(GROUP, width))
    upstream = core_major(norm_gain)[None, :] * (
        by_xor(group_rows.reshape(4, -1), x_index).reshape(GROUP, width) / SEQ
    )
    hidden_2 = [
        lax.ppermute(hidden_1[0], **xor("x", 4, 3)),
        lax.ppermute(hidden_3[1], **xor("x", 4, 1)),
    ]
    hidden_2 = jnp.stack(hidden_2)
    hidden = jnp.concatenate([hidden_0, hidden_1, hidden_2, hidden_3], axis=0).astype(F32)
    inverse = lax.rsqrt(jnp.mean(hidden * hidden, axis=2, keepdims=True) + NORM_EPS)
    inner = jnp.sum(upstream[:, None, :] * hidden, axis=2, keepdims=True) / width
    stream = inverse * upstream[:, None, :] - hidden * (inverse * inverse * inverse * inner)
    stream = stream.astype(BF16).reshape(tokens, width)

    cut = width // (2 * N_P)
    side = width // 2
    stream_other = swap(lax.dynamic_slice_in_dim(stream, (1 - core) * side, side, 1))
    stream_keep = lax.dynamic_slice_in_dim(stream, core * side, side, 1)
    weight = dot(stream_keep, attn, ((0,), (0,))) + dot(stream_other, attn_other, ((0,), (0,)))
    weight = weight.astype(BF16).reshape(N_P, cut, heads)
    final = jnp.concatenate([weight, jnp.broadcast_to(losses[None], (N_P, 8, heads))], axis=1)
    final = lax.all_to_all(final, PLANE, 0, 0)
    head_grad = dot(stream, out_proj, ((1,), (1,))).astype(BF16)
    head_grad = by_xor(head_grad.reshape(4, x_block, heads), x_index).reshape(tokens, heads)
    items_own = by_plane[:, :, :feats].reshape(half, feats)
    by_item = by_plane[:, :, feats:].reshape(N_P, rows, 2, rows).transpose(2, 0, 3, 1)
    by_item = by_item.reshape(2, half, rows)
    user_grad = (
        dot(by_item[0], items_own, ((0,), (0,))) + dot(by_item[1], swap(items_own), ((0,), (0,)))
    ) * LOGIT_SCALE
    weight_grad = jnp.sum(final[:, :cut].astype(F32), axis=0).T
    loss_mean = jnp.sum(final[:, cut].astype(F32)) / (2 * half)
    return (loss_mean, item_grad, user_grad, head_grad, weight_grad)


def solution(mesh):
    names, sizes = zip(*AXES)
    fine = Mesh(mesh.devices.reshape(sizes), names)
    both = P(DP, TENSOR)
    return jax.shard_map(
        per_device,
        mesh=fine,
        in_specs=(both, both, P(DP), both, P(DP, None), P(TENSOR, None), P()),
        out_specs=(P(), both, both, both, P(TENSOR, DP)),
        check_vma=False,
    )
```

```python
import jax
import jax.numpy as jnp
from jax import lax
from jax.experimental import pallas as pl
from jax.experimental.pallas import tpu as pltpu
from jax.sharding import Mesh, PartitionSpec as P

BF16 = jnp.bfloat16
F32 = jnp.float32
LOGIT_SCALE = 50.0
NORM_EPS = 1e-06
GROUP = 8
SEQ = 32
AXES = (("zl", 4), ("y", 8), ("c", 2), ("x", 4), ("zh", 2))
TENSOR = ("x", "zh")
PLANE = ("zl", "y")
DP = ("zl", "y", "c")
N_T = 8
N_P = 32


def xor(axis, size, bits):
    return dict(axis_name=axis, perm=[(i, i ^ bits) for i in range(size)])


def swap(value):
    return lax.ppermute(value, **xor("c", 2, 1))


def three_terms(value):
    high = lax.reduce_precision(value, 8, 7)
    rest = value - high
    middle = lax.reduce_precision(rest, 8, 7)
    low = lax.reduce_precision(rest - middle, 8, 7)
    return high.astype(BF16), middle.astype(BF16), low.astype(BF16)


def to_all(value, axes, count):
    return lax.all_to_all(jnp.broadcast_to(value[None], (count,) + value.shape), axes, 0, 0)


def dot(a, b, dims):
    return lax.dot_general(a, b, (dims, ((), ())), preferred_element_type=F32)


def by_xor(value, index):
    parts = [lax.dynamic_slice_in_dim(value, r ^ index, 1, 0) for r in range(value.shape[0])]
    return jnp.concatenate(parts, axis=0)


def tie(value, column):
    return value + (column * 0).astype(value.dtype)


def stream_kernel(x_ref, gain_ref, group_ref, *refs):
    first, second, third_0, third_1, fourth, out_ref = refs
    halves = (first, first, second, second, third_0, third_1, fourth, fourth)
    width = out_ref.shape[1]
    for item in range(GROUP):
        start = 0 if halves[item].shape[0] == SEQ else item % 2 * SEQ
        tokens = halves[item][start : start + SEQ, :].astype(F32)
        which = (x_ref[0] ^ (item // 2)) * 2 + item % 2
        up = gain_ref[...] * (group_ref[pl.ds(which, 1), :] / SEQ)
        mean = jnp.sum(tokens * tokens, axis=1, keepdims=True) / width
        inverse = lax.rsqrt(mean + NORM_EPS)
        inner = jnp.sum(up * tokens, axis=1, keepdims=True) / width
        stream = inverse * up - tokens * (inverse * inverse * inverse * inner)
        out_ref[item * SEQ : (item + 1) * SEQ, :] = stream.astype(BF16)


def stream_gradient(x_index, norm_gain, group_rows, blocks):
    tokens, width = GROUP * SEQ, norm_gain.shape[0]
    whole = pl.BlockSpec(memory_space=pltpu.VMEM)
    return pl.pallas_call(
        stream_kernel,
        out_shape=jax.ShapeDtypeStruct((tokens, width), BF16),
        in_specs=[pl.BlockSpec(memory_space=pltpu.SMEM)] + [whole] * 7,
        out_specs=whole,
        compiler_params=pltpu.CompilerParams(vmem_limit_bytes=24 * 2**20),
        cost_estimate=pl.CostEstimate(
            flops=12 * tokens * width, bytes_accessed=4 * tokens * width, transcendentals=0
        ),
    )(x_index.reshape(1), norm_gain.reshape(1, width), group_rows, *blocks)


def per_device(item_cache, user_cache, positive, attn_heads, residual, out_proj, norm_gain):
    rows, feats = item_cache.shape
    width = out_proj.shape[1]
    tokens, heads = attn_heads.shape
    half = N_P * rows
    core = lax.axis_index("c")
    x_index = lax.axis_index("x")
    z_index = lax.axis_index("zh")
    x_block = tokens // 4

    attn = by_xor(attn_heads.reshape(4, x_block, heads), x_index).reshape(tokens, heads)
    mixed = dot(attn, out_proj, ((1,), (0,))).astype(BF16)
    from_x = [
        lax.ppermute(mixed[k * x_block : (k + 1) * x_block], **xor("x", 4, k)) for k in (1, 2, 3)
    ]
    mixed_x = mixed[:x_block].astype(F32) + sum(part.astype(F32) for part in from_x)
    mixed_x = mixed_x.reshape(2, rows, width)
    mixed_give = lax.dynamic_index_in_dim(mixed_x, 1 - z_index, 0, keepdims=False)
    mixed_keep = lax.dynamic_index_in_dim(mixed_x, z_index, 0, keepdims=False)
    from_z = lax.ppermute(mixed_give.astype(BF16), **xor("zh", 2, 1))

    users_own = to_all(user_cache, PLANE, N_P).reshape(half, feats)
    users = (users_own, swap(users_own))

    partial = [dot(item_cache, u, ((1,), (1,))) for u in users]
    partial = jnp.concatenate(partial, axis=1)
    share = 2 * half // N_T
    partial = partial.reshape(rows, N_T, share).transpose(1, 0, 2)
    scores_own = jnp.sum(lax.all_to_all(partial, TENSOR, 0, 0), axis=0) * LOGIT_SCALE
    scores = to_all(scores_own, TENSOR, N_T).transpose(1, 0, 2).reshape(rows, 2 * half)

    own_residual = lax.dynamic_slice_in_dim(residual, (2 * x_index + z_index) * rows, rows, 0)
    hidden_own = tie(from_z.astype(F32), partial[0, :, :1]) + own_residual.astype(F32)
    hidden_own = (mixed_keep + hidden_own).astype(BF16)

    hidden_z = tie(lax.ppermute(hidden_own, **xor("zh", 2, 1)), scores_own[:, :1])
    hidden_0 = jnp.stack([hidden_own, hidden_z])
    hidden_0 = jnp.where(z_index == 0, hidden_0, hidden_0[::-1]).reshape(x_block, width)
    hidden_1 = lax.ppermute(hidden_0, **xor("x", 4, 1))
    hidden_3 = lax.ppermute(hidden_0, **xor("x", 4, 3))

    owner, row_in = positive // rows, positive % rows
    column = (owner % 2 != core).astype(jnp.int32) * half + (owner // 2) * rows + row_in
    maxima = jnp.max(scores, axis=1, keepdims=True)
    log_total = maxima[:, 0] + jnp.log(jnp.sum(jnp.exp(scores - maxima), axis=1))
    target = column[:, None] == lax.broadcasted_iota(jnp.int32, (1, 2 * half), 1)
    picked = jnp.sum(jnp.where(target, scores, F32(0.0)), axis=1)
    losses = jnp.concatenate(three_terms(log_total - picked))
    grad = (jnp.exp(scores - log_total[:, None]) - target.astype(F32)).astype(BF16)
    item_grad = (
        dot(grad[:, :half], users[0], ((1,), (0,))) + dot(grad[:, half:], users[1], ((1,), (0,)))
    ) * LOGIT_SCALE
    group_rows = to_all(item_grad[:GROUP], TENSOR, N_T)
    hidden_2 = [
        lax.ppermute(tie(hidden_1[:rows], item_grad[:, :1]), **xor("x", 4, 3)),
        lax.ppermute(tie(hidden_3[rows:], item_grad[:, :1]), **xor("x", 4, 1)),
    ]
    hidden = (hidden_0, hidden_1, *hidden_2, hidden_3)

    grad_losses = jnp.zeros((8, half), BF16).at[0, : 3 * rows].set(losses)
    other = swap(jnp.concatenate([grad[:, half:], grad_losses], axis=0))
    losses = jnp.concatenate([losses, other[rows, : 3 * rows]])
    losses = jnp.pad(losses, (0, 2 * rows)).reshape(2, heads // 2)
    losses = jnp.pad(losses, ((0, 6), (0, 0)))
    both = jnp.concatenate([grad[:, :half], other[:rows]], axis=0)
    both = both.T.reshape(N_P, rows, 2 * rows)
    by_plane = jnp.concatenate(
        [jnp.broadcast_to(item_cache[None], (N_P, rows, feats)), both], axis=2
    )
    by_plane = lax.all_to_all(by_plane, PLANE, 0, 0)

    group_rows = group_rows.transpose(1, 0, 2).reshape(GROUP, width)
    stream = stream_gradient(x_index, norm_gain, group_rows, hidden)

    side = heads // 2
    cut = width // N_P
    attn_give = lax.dynamic_slice_in_dim(attn, (1 - core) * side, side, 1)
    attn_keep = lax.dynamic_slice_in_dim(attn, core * side, side, 1)
    weight_give = swap(dot(stream, attn_give, ((0,), (0,))).astype(BF16))
    weight = dot(stream, attn_keep, ((0,), (0,))) + weight_give.astype(F32)
    weight = weight.astype(BF16).reshape(N_P, cut, side)
    final = jnp.concatenate([weight, jnp.broadcast_to(losses[None], (N_P, 8, side))], axis=1)
    final = lax.all_to_all(final, PLANE, 0, 0)
    head_grad = dot(stream, out_proj, ((1,), (1,))).astype(BF16)
    head_grad = by_xor(head_grad.reshape(4, x_block, heads), x_index).reshape(tokens, heads)
    items_own = by_plane[:, :, :feats].reshape(half, feats)
    by_item = by_plane[:, :, feats:].reshape(N_P, rows, 2, rows).transpose(2, 0, 3, 1)
    by_item = by_item.reshape(2, half, rows)
    user_grad = (
        dot(by_item[0], items_own, ((0,), (0,))) + dot(by_item[1], swap(items_own), ((0,), (0,)))
    ) * LOGIT_SCALE
    weight = jnp.sum(final[:, :cut].astype(F32), axis=0).reshape(2, cut // 2, side)
    weight_keep = lax.dynamic_index_in_dim(weight, core, 0, keepdims=False)
    weight_other = swap(lax.dynamic_index_in_dim(weight, 1 - core, 0, keepdims=False))
    lower = jnp.where(core == 0, weight_keep, weight_other)
    upper = jnp.where(core == 0, weight_other, weight_keep)
    weight_grad = jnp.concatenate([lower, upper], axis=1).T
    loss_mean = jnp.sum(final[:, cut:].astype(F32)) / (2 * half)
    return (loss_mean, item_grad, user_grad, head_grad, weight_grad)


def solution(mesh):
    names, sizes = zip(*AXES)
    fine = Mesh(mesh.devices.reshape(sizes), names)
    both = P(DP, TENSOR)
    return jax.shard_map(
        per_device,
        mesh=fine,
        in_specs=(both, both, P(DP), both, P(DP, None), P(TENSOR, None), P()),
        out_specs=(P(), both, both, both, P(TENSOR, DP)),
        check_vma=False,
    )
```

```python
import jax
import jax.numpy as jnp
from jax import lax
from jax.experimental import pallas as pl
from jax.experimental.pallas import tpu as pltpu
from jax.sharding import Mesh, PartitionSpec as P

BF16 = jnp.bfloat16
F32 = jnp.float32
LOGIT_SCALE = 50.0
NORM_EPS = 1e-06
GROUP = 8
SEQ = 32
AXES = (("zl", 4), ("y", 8), ("c", 2), ("x", 4), ("zh", 2))
TENSOR = ("x", "zh")
PLANE = ("zl", "y")
DP = ("zl", "y", "c")
N_T = 8
N_P = 32


def xor(axis, size, bits):
    return dict(axis_name=axis, perm=[(i, i ^ bits) for i in range(size)])


def swap(value):
    return lax.ppermute(value, **xor("c", 2, 1))


def three_terms(value):
    high = lax.reduce_precision(value, 8, 7)
    rest = value - high
    middle = lax.reduce_precision(rest, 8, 7)
    low = lax.reduce_precision(rest - middle, 8, 7)
    return high.astype(BF16), middle.astype(BF16), low.astype(BF16)


def to_all(value, axes, count):
    return lax.all_to_all(jnp.broadcast_to(value[None], (count,) + value.shape), axes, 0, 0)


def dot(a, b, dims):
    return lax.dot_general(a, b, (dims, ((), ())), preferred_element_type=F32)


def by_xor(value, index):
    parts = [lax.dynamic_slice_in_dim(value, r ^ index, 1, 0) for r in range(value.shape[0])]
    return jnp.concatenate(parts, axis=0)


def tie(value, column):
    return value + (column * 0).astype(value.dtype)


def stream_kernel(x_ref, group_ref, *refs):
    first, second, third_0, third_1, fourth, out_ref, up_ref = refs
    halves = (first, first, second, second, third_0, third_1, fourth, fourth)
    width = out_ref.shape[1]
    up_ref[...] = jnp.concatenate([group_ref[t] for t in range(N_T)], axis=1)
    for item in range(GROUP):
        start = 0 if halves[item].shape[0] == SEQ else item % 2 * SEQ
        tokens = halves[item][start : start + SEQ, :].astype(F32)
        which = (x_ref[0] ^ (item // 2)) * 2 + item % 2
        up = up_ref[pl.ds(which, 1), :]
        mean = jnp.sum(tokens * tokens, axis=1, keepdims=True) / width
        inverse = lax.rsqrt(mean + NORM_EPS)
        inner = jnp.sum(up * tokens, axis=1, keepdims=True) / width
        stream = inverse * up - tokens * (inverse * inverse * inverse * inner)
        out_ref[item * SEQ : (item + 1) * SEQ, :] = stream.astype(BF16)


def stream_gradient(x_index, group_rows, blocks):
    tokens, width = GROUP * SEQ, blocks[0].shape[1]
    whole = pl.BlockSpec(memory_space=pltpu.VMEM)
    return pl.pallas_call(
        stream_kernel,
        out_shape=jax.ShapeDtypeStruct((tokens, width), BF16),
        in_specs=[pl.BlockSpec(memory_space=pltpu.SMEM)] + [whole] * 6,
        out_specs=whole,
        scratch_shapes=[pltpu.VMEM((GROUP, width), F32)],
        compiler_params=pltpu.CompilerParams(vmem_limit_bytes=24 * 2**20),
        cost_estimate=pl.CostEstimate(
            flops=12 * tokens * width, bytes_accessed=4 * tokens * width, transcendentals=0
        ),
    )(x_index.reshape(1), group_rows, *blocks)


def payload_kernel(item_ref, own_ref, other_ref, out_ref):
    rows, feats = item_ref.shape
    both = jnp.concatenate([own_ref[...].astype(F32), other_ref[:rows, :].astype(F32)], axis=0)
    both = both.T.astype(BF16)
    for place in range(N_P):
        out_ref[place, :, :feats] = item_ref[...]
        out_ref[place, :, feats:] = both[place * rows : (place + 1) * rows, :]


def plane_payload(item_cache, own, other):
    rows, feats = item_cache.shape
    whole = pl.BlockSpec(memory_space=pltpu.VMEM)
    size = N_P * rows * (feats + 2 * rows)
    return pl.pallas_call(
        payload_kernel,
        out_shape=jax.ShapeDtypeStruct((N_P, rows, feats + 2 * rows), BF16),
        in_specs=[whole] * 3,
        out_specs=whole,
        compiler_params=pltpu.CompilerParams(vmem_limit_bytes=12 * 2**20),
        cost_estimate=pl.CostEstimate(flops=0, bytes_accessed=2 * size, transcendentals=0),
    )(item_cache, own, other)


def per_device(item_cache, user_cache, positive, attn_heads, residual, out_proj, norm_gain):
    rows, feats = item_cache.shape
    width = out_proj.shape[1]
    tokens, heads = attn_heads.shape
    half = N_P * rows
    core = lax.axis_index("c")
    x_index = lax.axis_index("x")
    z_index = lax.axis_index("zh")
    x_block = tokens // 4

    attn = by_xor(attn_heads.reshape(4, x_block, heads), x_index).reshape(tokens, heads)
    mixed = dot(attn, out_proj, ((1,), (0,))).astype(BF16)
    from_x = [
        lax.ppermute(mixed[k * x_block : (k + 1) * x_block], **xor("x", 4, k)) for k in (1, 2, 3)
    ]
    mixed_x = mixed[:x_block].astype(F32) + sum(part.astype(F32) for part in from_x)
    mixed_x = mixed_x.reshape(2, rows, width)
    mixed_give = lax.dynamic_index_in_dim(mixed_x, 1 - z_index, 0, keepdims=False)
    mixed_keep = lax.dynamic_index_in_dim(mixed_x, z_index, 0, keepdims=False)
    from_z = lax.ppermute(mixed_give.astype(BF16), **xor("zh", 2, 1))

    users_own = to_all(user_cache, PLANE, N_P).reshape(half, feats)
    users = (users_own, swap(users_own))

    partial = [dot(item_cache, u, ((1,), (1,))) for u in users]
    partial = jnp.concatenate(partial, axis=1)
    share = 2 * half // N_T
    partial = partial.reshape(rows, N_T, share).transpose(1, 0, 2)
    scores_own = jnp.sum(lax.all_to_all(partial, TENSOR, 0, 0), axis=0) * LOGIT_SCALE
    scores = to_all(scores_own, TENSOR, N_T).transpose(1, 0, 2).reshape(rows, 2 * half)

    own_residual = lax.dynamic_slice_in_dim(residual, (2 * x_index + z_index) * rows, rows, 0)
    hidden_own = tie(from_z.astype(F32), partial[0, :, :1]) + own_residual.astype(F32)
    hidden_own = (mixed_keep + hidden_own).astype(BF16)

    hidden_z = tie(lax.ppermute(hidden_own, **xor("zh", 2, 1)), scores_own[:, :1])
    hidden_0 = jnp.stack([hidden_own, hidden_z])
    hidden_0 = jnp.where(z_index == 0, hidden_0, hidden_0[::-1]).reshape(x_block, width)
    hidden_1 = lax.ppermute(hidden_0, **xor("x", 4, 1))
    hidden_3 = lax.ppermute(hidden_0, **xor("x", 4, 3))

    owner, row_in = positive // rows, positive % rows
    column = (owner % 2 != core).astype(jnp.int32) * half + (owner // 2) * rows + row_in
    maxima = jnp.max(scores, axis=1, keepdims=True)
    log_total = maxima[:, 0] + jnp.log(jnp.sum(jnp.exp(scores - maxima), axis=1))
    target = column[:, None] == lax.broadcasted_iota(jnp.int32, (1, 2 * half), 1)
    picked = jnp.sum(jnp.where(target, scores, F32(0.0)), axis=1)
    losses = jnp.concatenate(three_terms(log_total - picked))
    grad = (jnp.exp(scores - log_total[:, None]) - target.astype(F32)).astype(BF16)
    item_grad = (
        dot(grad[:, :half], users[0], ((1,), (0,))) + dot(grad[:, half:], users[1], ((1,), (0,)))
    ) * LOGIT_SCALE
    t_index = 2 * x_index + z_index
    own_gain = lax.dynamic_slice_in_dim(norm_gain, t_index * feats, feats, 0) / SEQ
    group_rows = to_all(own_gain[None, :] * item_grad[:GROUP], TENSOR, N_T)
    hidden_2 = [
        lax.ppermute(tie(hidden_1[:rows], item_grad[:, :1]), **xor("x", 4, 3)),
        lax.ppermute(tie(hidden_3[rows:], item_grad[:, :1]), **xor("x", 4, 1)),
    ]
    hidden = (hidden_0, hidden_1, *hidden_2, hidden_3)

    grad_losses = jnp.zeros((8, half), BF16).at[0, : 3 * rows].set(losses)
    other = swap(jnp.concatenate([grad[:, half:], grad_losses], axis=0))
    losses = jnp.concatenate([losses, other[rows, : 3 * rows]])
    losses = jnp.pad(losses, (0, 2 * rows)).reshape(2, heads // 2)
    losses = jnp.pad(losses, ((0, 6), (0, 0)))
    by_plane = plane_payload(item_cache, grad[:, :half], other)
    by_plane = lax.all_to_all(by_plane, PLANE, 0, 0)

    stream = stream_gradient(x_index, group_rows, hidden)

    side = heads // 2
    cut = width // N_P
    attn_give = lax.dynamic_slice_in_dim(attn, (1 - core) * side, side, 1)
    attn_keep = lax.dynamic_slice_in_dim(attn, core * side, side, 1)
    weight_give = swap(dot(stream, attn_give, ((0,), (0,))).astype(BF16))
    weight = dot(stream, attn_keep, ((0,), (0,))) + weight_give.astype(F32)
    weight = weight.astype(BF16).reshape(N_P, cut, side)
    final = jnp.concatenate([weight, jnp.broadcast_to(losses[None], (N_P, 8, side))], axis=1)
    final = lax.all_to_all(final, PLANE, 0, 0)
    head_grad = dot(stream, out_proj, ((1,), (1,))).astype(BF16)
    head_grad = by_xor(head_grad.reshape(4, x_block, heads), x_index).reshape(tokens, heads)
    items_own = by_plane[:, :, :feats].reshape(half, feats)
    by_item = by_plane[:, :, feats:].reshape(N_P, rows, 2, rows).transpose(2, 0, 3, 1)
    by_item = by_item.reshape(2, half, rows)
    user_grad = (
        dot(by_item[0], items_own, ((0,), (0,))) + dot(by_item[1], swap(items_own), ((0,), (0,)))
    ) * LOGIT_SCALE
    weight = jnp.sum(final[:, :cut].astype(F32), axis=0).reshape(2, cut // 2, side)
    weight_keep = lax.dynamic_index_in_dim(weight, core, 0, keepdims=False)
    weight_other = swap(lax.dynamic_index_in_dim(weight, 1 - core, 0, keepdims=False))
    lower = jnp.where(core == 0, weight_keep, weight_other)
    upper = jnp.where(core == 0, weight_other, weight_keep)
    weight_grad = jnp.concatenate([lower, upper], axis=1).T
    loss_mean = jnp.sum(final[:, cut:].astype(F32)) / (2 * half)
    return (loss_mean, item_grad, user_grad, head_grad, weight_grad)


def solution(mesh):
    names, sizes = zip(*AXES)
    fine = Mesh(mesh.devices.reshape(sizes), names)
    both = P(DP, TENSOR)
    return jax.shard_map(
        per_device,
        mesh=fine,
        in_specs=(both, both, P(DP), both, P(DP, None), P(TENSOR, None), P()),
        out_specs=(P(), both, both, both, P(TENSOR, DP)),
        check_vma=False,
    )
```

```python
import jax
import jax.numpy as jnp
from jax import lax
from jax.experimental import pallas as pl
from jax.experimental.pallas import tpu as pltpu
from jax.sharding import Mesh, PartitionSpec as P

BF16 = jnp.bfloat16
F32 = jnp.float32
LOGIT_SCALE = 50.0
NORM_EPS = 1e-06
GROUP = 8
SEQ = 32
AXES = (("zl", 4), ("y", 8), ("c", 2), ("x", 4), ("zh", 2))
TENSOR = ("x", "zh")
PLANE = ("zl", "y")
DP = ("zl", "y", "c")
N_T = 8
N_P = 32


def xor(axis, size, bits):
    return dict(axis_name=axis, perm=[(i, i ^ bits) for i in range(size)])


def swap(value):
    return lax.ppermute(value, **xor("c", 2, 1))


def to_all(value, axes, count):
    return lax.all_to_all(jnp.broadcast_to(value[None], (count,) + value.shape), axes, 0, 0)


def dot(a, b, dims):
    return lax.dot_general(a, b, (dims, ((), ())), preferred_element_type=F32)


def by_xor(value, index):
    parts = [lax.dynamic_slice_in_dim(value, r ^ index, 1, 0) for r in range(value.shape[0])]
    return jnp.concatenate(parts, axis=0)


def tie(value, column):
    return value + (column * 0).astype(value.dtype)


def stream_kernel(x_ref, group_ref, *refs):
    first, second, third_0, third_1, fourth, out_ref, up_ref = refs
    halves = (first, first, second, second, third_0, third_1, fourth, fourth)
    width = out_ref.shape[1]
    up_ref[...] = jnp.concatenate([group_ref[t] for t in range(N_T)], axis=1)
    for item in range(GROUP):
        start = 0 if halves[item].shape[0] == SEQ else item % 2 * SEQ
        tokens = halves[item][start : start + SEQ, :].astype(F32)
        which = (x_ref[0] ^ (item // 2)) * 2 + item % 2
        up = up_ref[pl.ds(which, 1), :]
        mean = jnp.sum(tokens * tokens, axis=1, keepdims=True) / width
        inverse = lax.rsqrt(mean + NORM_EPS)
        inner = jnp.sum(up * tokens, axis=1, keepdims=True) / width
        stream = inverse * up - tokens * (inverse * inverse * inverse * inner)
        out_ref[item * SEQ : (item + 1) * SEQ, :] = stream.astype(BF16)


def stream_gradient(x_index, group_rows, blocks):
    tokens, width = GROUP * SEQ, blocks[0].shape[1]
    whole = pl.BlockSpec(memory_space=pltpu.VMEM)
    return pl.pallas_call(
        stream_kernel,
        out_shape=jax.ShapeDtypeStruct((tokens, width), BF16),
        in_specs=[pl.BlockSpec(memory_space=pltpu.SMEM)] + [whole] * 6,
        out_specs=whole,
        scratch_shapes=[pltpu.VMEM((GROUP, width), F32)],
        compiler_params=pltpu.CompilerParams(vmem_limit_bytes=24 * 2**20),
        cost_estimate=pl.CostEstimate(
            flops=12 * tokens * width, bytes_accessed=4 * tokens * width, transcendentals=0
        ),
    )(x_index.reshape(1), group_rows, *blocks)


def softmax_kernel(score_ref, column_ref, own_ref, give_ref):
    rows, half = own_ref.shape
    scores = jnp.concatenate([score_ref[t] for t in range(N_T)], axis=1)
    lane = lax.broadcasted_iota(jnp.int32, scores.shape, 1)
    target = column_ref[...] == lane
    top = jnp.max(scores, axis=1, keepdims=True)
    log_total = top + jnp.log(jnp.sum(jnp.exp(scores - top), axis=1, keepdims=True))
    picked = jnp.sum(jnp.where(target, scores, F32(0.0)), axis=1, keepdims=True)
    grad = (jnp.exp(scores - log_total) - target.astype(F32)).astype(BF16)
    own_ref[...] = grad[:, :half]
    give_ref[:rows, :] = grad[:, half:]
    across = lax.broadcasted_iota(jnp.int32, (rows, half), 1)
    down = lax.broadcasted_iota(jnp.int32, (rows, half), 0)
    loss = jnp.where(across == down, log_total - picked, F32(0.0))
    loss = jnp.sum(loss, axis=0, keepdims=True)
    high = loss.astype(BF16).astype(F32)
    middle = (loss - high).astype(BF16).astype(F32)
    low = loss - high - middle
    row = lax.broadcasted_iota(jnp.int32, (16, half), 0)
    terms = jnp.where(row == 0, high, jnp.where(row == 1, middle, low))
    give_ref[rows:, :] = jnp.where(row < 3, terms, F32(0.0)).astype(BF16)


def softmax_gradient(scores, column):
    rows = scores.shape[1]
    half = N_T * scores.shape[2] // 2
    whole = pl.BlockSpec(memory_space=pltpu.VMEM)
    return pl.pallas_call(
        softmax_kernel,
        out_shape=(
            jax.ShapeDtypeStruct((rows, half), BF16),
            jax.ShapeDtypeStruct((rows + 16, half), BF16),
        ),
        in_specs=[whole] * 2,
        out_specs=(whole, whole),
        compiler_params=pltpu.CompilerParams(vmem_limit_bytes=12 * 2**20),
        cost_estimate=pl.CostEstimate(
            flops=16 * rows * half, bytes_accessed=12 * rows * half, transcendentals=4 * rows * half
        ),
    )(scores, column[:, None])


def payload_kernel(item_ref, own_ref, other_ref, out_ref):
    rows, feats = item_ref.shape
    both = jnp.concatenate([own_ref[...].astype(F32), other_ref[:rows, :].astype(F32)], axis=0)
    both = both.T.astype(BF16)
    for place in range(N_P):
        out_ref[place, :, :feats] = item_ref[...]
        out_ref[place, :, feats:] = both[place * rows : (place + 1) * rows, :]


def plane_payload(item_cache, own, other):
    rows, feats = item_cache.shape
    whole = pl.BlockSpec(memory_space=pltpu.VMEM)
    size = N_P * rows * (feats + 2 * rows)
    return pl.pallas_call(
        payload_kernel,
        out_shape=jax.ShapeDtypeStruct((N_P, rows, feats + 2 * rows), BF16),
        in_specs=[whole] * 3,
        out_specs=whole,
        compiler_params=pltpu.CompilerParams(vmem_limit_bytes=12 * 2**20),
        cost_estimate=pl.CostEstimate(flops=0, bytes_accessed=2 * size, transcendentals=0),
    )(item_cache, own, other)


def per_device(item_cache, user_cache, positive, attn_heads, residual, out_proj, norm_gain):
    rows, feats = item_cache.shape
    width = out_proj.shape[1]
    tokens, heads = attn_heads.shape
    half = N_P * rows
    core = lax.axis_index("c")
    x_index = lax.axis_index("x")
    z_index = lax.axis_index("zh")
    x_block = tokens // 4

    attn = by_xor(attn_heads.reshape(4, x_block, heads), x_index).reshape(tokens, heads)
    mixed = dot(attn, out_proj, ((1,), (0,))).astype(BF16)
    from_x = [
        lax.ppermute(mixed[k * x_block : (k + 1) * x_block], **xor("x", 4, k)) for k in (1, 2, 3)
    ]
    mixed_x = mixed[:x_block].astype(F32) + sum(part.astype(F32) for part in from_x)
    mixed_x = mixed_x.reshape(2, rows, width)
    mixed_give = lax.dynamic_index_in_dim(mixed_x, 1 - z_index, 0, keepdims=False)
    mixed_keep = lax.dynamic_index_in_dim(mixed_x, z_index, 0, keepdims=False)
    from_z = lax.ppermute(mixed_give.astype(BF16), **xor("zh", 2, 1))

    users_own = to_all(user_cache, PLANE, N_P).reshape(half, feats)
    users = (users_own, swap(users_own))

    partial = [dot(item_cache, u, ((1,), (1,))) for u in users]
    partial = jnp.concatenate(partial, axis=1)
    share = 2 * half // N_T
    partial = partial.reshape(rows, N_T, share).transpose(1, 0, 2)
    scores_own = jnp.sum(lax.all_to_all(partial, TENSOR, 0, 0), axis=0) * LOGIT_SCALE
    scores = to_all(scores_own, TENSOR, N_T)

    own_residual = lax.dynamic_slice_in_dim(residual, (2 * x_index + z_index) * rows, rows, 0)
    hidden_own = tie(from_z.astype(F32), partial[0, :, :1]) + own_residual.astype(F32)
    hidden_own = (mixed_keep + hidden_own).astype(BF16)

    hidden_z = tie(lax.ppermute(hidden_own, **xor("zh", 2, 1)), scores_own[:, :1])
    hidden_0 = jnp.stack([hidden_own, hidden_z])
    hidden_0 = jnp.where(z_index == 0, hidden_0, hidden_0[::-1]).reshape(x_block, width)
    hidden_1 = lax.ppermute(hidden_0, **xor("x", 4, 1))
    hidden_3 = lax.ppermute(hidden_0, **xor("x", 4, 3))

    owner, row_in = positive // rows, positive % rows
    column = (owner % 2 != core).astype(jnp.int32) * half + (owner // 2) * rows + row_in
    grad_own, grad_give = softmax_gradient(scores, column)
    item_grad = (
        dot(grad_own, users[0], ((1,), (0,))) + dot(grad_give[:rows], users[1], ((1,), (0,)))
    ) * LOGIT_SCALE
    t_index = 2 * x_index + z_index
    own_gain = lax.dynamic_slice_in_dim(norm_gain, t_index * feats, feats, 0) / SEQ
    group_rows = to_all(own_gain[None, :] * item_grad[:GROUP], TENSOR, N_T)
    hidden_2 = [
        lax.ppermute(tie(hidden_1[:rows], item_grad[:, :1]), **xor("x", 4, 3)),
        lax.ppermute(tie(hidden_3[rows:], item_grad[:, :1]), **xor("x", 4, 1)),
    ]
    hidden = (hidden_0, hidden_1, *hidden_2, hidden_3)

    other = swap(grad_give)
    losses = jnp.concatenate([part[rows : rows + 3, : heads // 2] for part in (grad_give, other)])
    losses = jnp.pad(losses, ((0, 2), (0, 0)))
    by_plane = plane_payload(item_cache, grad_own, other)
    by_plane = lax.all_to_all(by_plane, PLANE, 0, 0)

    stream = stream_gradient(x_index, group_rows, hidden)

    side = heads // 2
    cut = width // N_P
    attn_give = lax.dynamic_slice_in_dim(attn, (1 - core) * side, side, 1)
    attn_keep = lax.dynamic_slice_in_dim(attn, core * side, side, 1)
    weight_give = swap(dot(stream, attn_give, ((0,), (0,))).astype(BF16))
    weight = dot(stream, attn_keep, ((0,), (0,))) + weight_give.astype(F32)
    weight = weight.astype(BF16).reshape(N_P, cut, side)
    final = jnp.concatenate([weight, jnp.broadcast_to(losses[None], (N_P, 8, side))], axis=1)
    final = lax.all_to_all(final, PLANE, 0, 0)
    head_grad = dot(stream, out_proj, ((1,), (1,))).astype(BF16)
    head_grad = by_xor(head_grad.reshape(4, x_block, heads), x_index).reshape(tokens, heads)
    items_own = by_plane[:, :, :feats].reshape(half, feats)
    by_item = by_plane[:, :, feats:].reshape(N_P, rows, 2, rows).transpose(2, 0, 3, 1)
    by_item = by_item.reshape(2, half, rows)
    user_grad = (
        dot(by_item[0], items_own, ((0,), (0,))) + dot(by_item[1], swap(items_own), ((0,), (0,)))
    ) * LOGIT_SCALE
    weight = jnp.sum(final[:, :cut].astype(F32), axis=0).reshape(2, cut // 2, side)
    weight_keep = lax.dynamic_index_in_dim(weight, core, 0, keepdims=False)
    weight_other = swap(lax.dynamic_index_in_dim(weight, 1 - core, 0, keepdims=False))
    lower = jnp.where(core == 0, weight_keep, weight_other)
    upper = jnp.where(core == 0, weight_other, weight_keep)
    weight_grad = jnp.concatenate([lower, upper], axis=1).T
    loss_mean = jnp.sum(final[:, cut:].astype(F32)) / (2 * half)
    return (loss_mean, item_grad, user_grad, head_grad, weight_grad)


def solution(mesh):
    names, sizes = zip(*AXES)
    fine = Mesh(mesh.devices.reshape(sizes), names)
    both = P(DP, TENSOR)
    return jax.shard_map(
        per_device,
        mesh=fine,
        in_specs=(both, both, P(DP), both, P(DP, None), P(TENSOR, None), P()),
        out_specs=(P(), both, both, both, P(TENSOR, DP)),
        check_vma=False,
    )
```

```python
import jax
import jax.numpy as jnp
from jax import lax
from jax.experimental import pallas as pl
from jax.experimental.pallas import tpu as pltpu
from jax.sharding import Mesh, PartitionSpec as P

BF16 = jnp.bfloat16
F32 = jnp.float32
LOGIT_SCALE = 50.0
NORM_EPS = 1e-06
GROUP = 8
SEQ = 32
AXES = (("zl", 4), ("y", 8), ("c", 2), ("x", 4), ("zh", 2))
TENSOR = ("x", "zh")
PLANE = ("zl", "y")
DP = ("zl", "y", "c")
N_T = 8
N_P = 32


def xor(axis, size, bits):
    return dict(axis_name=axis, perm=[(i, i ^ bits) for i in range(size)])


def swap(value):
    return lax.ppermute(value, **xor("c", 2, 1))


def to_all(value, axes, count):
    return lax.all_to_all(jnp.broadcast_to(value[None], (count,) + value.shape), axes, 0, 0)


def dot(a, b, dims):
    return lax.dot_general(a, b, (dims, ((), ())), preferred_element_type=F32)


def by_xor(value, index):
    parts = [lax.dynamic_slice_in_dim(value, r ^ index, 1, 0) for r in range(value.shape[0])]
    return jnp.concatenate(parts, axis=0)


def tie(value, column):
    return value + (column * 0).astype(value.dtype)


def stream_kernel(x_ref, group_ref, *refs):
    first, second, third_0, third_1, fourth, out_ref, up_ref = refs
    halves = (first, first, second, second, third_0, third_1, fourth, fourth)
    width = out_ref.shape[1]
    up_ref[...] = jnp.concatenate([group_ref[t] for t in range(N_T)], axis=1)
    for item in range(GROUP):
        start = 0 if halves[item].shape[0] == SEQ else item % 2 * SEQ
        tokens = halves[item][start : start + SEQ, :].astype(F32)
        which = (x_ref[0] ^ (item // 2)) * 2 + item % 2
        up = up_ref[pl.ds(which, 1), :]
        mean = jnp.sum(tokens * tokens, axis=1, keepdims=True) / width
        inverse = lax.rsqrt(mean + NORM_EPS)
        inner = jnp.sum(up * tokens, axis=1, keepdims=True) / width
        stream = inverse * up - tokens * (inverse * inverse * inverse * inner)
        out_ref[item * SEQ : (item + 1) * SEQ, :] = stream.astype(BF16)


def stream_gradient(x_index, group_rows, blocks):
    tokens, width = GROUP * SEQ, blocks[0].shape[1]
    whole = pl.BlockSpec(memory_space=pltpu.VMEM)
    return pl.pallas_call(
        stream_kernel,
        out_shape=jax.ShapeDtypeStruct((tokens, width), BF16),
        in_specs=[pl.BlockSpec(memory_space=pltpu.SMEM)] + [whole] * 6,
        out_specs=whole,
        scratch_shapes=[pltpu.VMEM((GROUP, width), F32)],
        compiler_params=pltpu.CompilerParams(vmem_limit_bytes=24 * 2**20),
        cost_estimate=pl.CostEstimate(
            flops=12 * tokens * width, bytes_accessed=4 * tokens * width, transcendentals=0
        ),
    )(x_index.reshape(1), group_rows, *blocks)


def score_kernel(part_ref, out_ref):
    total = part_ref[0]
    for t in range(1, N_T):
        total += part_ref[t]
    for t in range(N_T):
        out_ref[t] = total * LOGIT_SCALE


def score_sum(parts):
    whole = pl.BlockSpec(memory_space=pltpu.VMEM)
    return pl.pallas_call(
        score_kernel,
        out_shape=jax.ShapeDtypeStruct(parts.shape, F32),
        in_specs=[whole],
        out_specs=whole,
        compiler_params=pltpu.CompilerParams(vmem_limit_bytes=12 * 2**20),
        cost_estimate=pl.CostEstimate(
            flops=parts.size, bytes_accessed=8 * parts.size, transcendentals=0
        ),
    )(parts)


def softmax_kernel(
    score_ref, column_ref, gain_ref, near_ref, far_ref, own_ref, give_ref, item_ref, group_ref
):
    rows, half = own_ref.shape
    scores = jnp.concatenate([score_ref[t] for t in range(N_T)], axis=1)
    lane = lax.broadcasted_iota(jnp.int32, scores.shape, 1)
    target = column_ref[...] == lane
    top = jnp.max(scores, axis=1, keepdims=True)
    log_total = top + jnp.log(jnp.sum(jnp.exp(scores - top), axis=1, keepdims=True))
    picked = jnp.sum(jnp.where(target, scores, F32(0.0)), axis=1, keepdims=True)
    grad = (jnp.exp(scores - log_total) - target.astype(F32)).astype(BF16)
    own_ref[...] = grad[:, :half]
    give_ref[:rows, :] = grad[:, half:]
    item = dot(grad[:, :half], near_ref[...], ((1,), (0,)))
    item = (item + dot(grad[:, half:], far_ref[...], ((1,), (0,)))) * LOGIT_SCALE
    item_ref[...] = item
    for t in range(N_T):
        group_ref[t] = gain_ref[...] * item[:GROUP, :]
    across = lax.broadcasted_iota(jnp.int32, (rows, half), 1)
    down = lax.broadcasted_iota(jnp.int32, (rows, half), 0)
    loss = jnp.where(across == down, log_total - picked, F32(0.0))
    loss = jnp.sum(loss, axis=0, keepdims=True)
    high = loss.astype(BF16).astype(F32)
    middle = (loss - high).astype(BF16).astype(F32)
    low = loss - high - middle
    row = lax.broadcasted_iota(jnp.int32, (16, half), 0)
    terms = jnp.where(row == 0, high, jnp.where(row == 1, middle, low))
    give_ref[rows:, :] = jnp.where(row < 3, terms, F32(0.0)).astype(BF16)


def softmax_gradient(scores, column, gain, users):
    rows, feats = scores.shape[1], gain.shape[0]
    half = N_T * scores.shape[2] // 2
    whole = pl.BlockSpec(memory_space=pltpu.VMEM)
    return pl.pallas_call(
        softmax_kernel,
        out_shape=(
            jax.ShapeDtypeStruct((rows, half), BF16),
            jax.ShapeDtypeStruct((rows + 16, half), BF16),
            jax.ShapeDtypeStruct((rows, feats), F32),
            jax.ShapeDtypeStruct((N_T, GROUP, feats), F32),
        ),
        in_specs=[whole] * 5,
        out_specs=(whole,) * 4,
        compiler_params=pltpu.CompilerParams(vmem_limit_bytes=16 * 2**20),
        cost_estimate=pl.CostEstimate(
            flops=4 * rows * half * feats, bytes_accessed=12 * rows * half, transcendentals=4 * rows * half
        ),
    )(scores, column[:, None], gain[None, :], *users)


def payload_kernel(item_ref, own_ref, other_ref, out_ref):
    rows, feats = item_ref.shape
    both = jnp.concatenate([own_ref[...].astype(F32), other_ref[:rows, :].astype(F32)], axis=0)
    both = both.T.astype(BF16)
    for place in range(N_P):
        out_ref[place, :, :feats] = item_ref[...]
        out_ref[place, :, feats:] = both[place * rows : (place + 1) * rows, :]


def plane_payload(item_cache, own, other):
    rows, feats = item_cache.shape
    whole = pl.BlockSpec(memory_space=pltpu.VMEM)
    size = N_P * rows * (feats + 2 * rows)
    return pl.pallas_call(
        payload_kernel,
        out_shape=jax.ShapeDtypeStruct((N_P, rows, feats + 2 * rows), BF16),
        in_specs=[whole] * 3,
        out_specs=whole,
        compiler_params=pltpu.CompilerParams(vmem_limit_bytes=12 * 2**20),
        cost_estimate=pl.CostEstimate(flops=0, bytes_accessed=2 * size, transcendentals=0),
    )(item_cache, own, other)


def per_device(item_cache, user_cache, positive, attn_heads, residual, out_proj, norm_gain):
    rows, feats = item_cache.shape
    width = out_proj.shape[1]
    tokens, heads = attn_heads.shape
    half = N_P * rows
    core = lax.axis_index("c")
    x_index = lax.axis_index("x")
    z_index = lax.axis_index("zh")
    x_block = tokens // 4

    attn = by_xor(attn_heads.reshape(4, x_block, heads), x_index).reshape(tokens, heads)
    mixed = dot(attn, out_proj, ((1,), (0,))).astype(BF16)
    from_x = [
        lax.ppermute(mixed[k * x_block : (k + 1) * x_block], **xor("x", 4, k)) for k in (1, 2, 3)
    ]
    mixed_x = mixed[:x_block].astype(F32) + sum(part.astype(F32) for part in from_x)
    mixed_x = mixed_x.reshape(2, rows, width)
    mixed_give = lax.dynamic_index_in_dim(mixed_x, 1 - z_index, 0, keepdims=False)
    mixed_keep = lax.dynamic_index_in_dim(mixed_x, z_index, 0, keepdims=False)
    from_z = lax.ppermute(mixed_give.astype(BF16), **xor("zh", 2, 1))

    users_own = to_all(user_cache, PLANE, N_P).reshape(half, feats)
    users = (users_own, swap(users_own))

    partial = [dot(item_cache, u, ((1,), (1,))) for u in users]
    partial = jnp.concatenate(partial, axis=1)
    share = 2 * half // N_T
    partial = partial.reshape(rows, N_T, share).transpose(1, 0, 2)
    scores_own = score_sum(lax.all_to_all(partial, TENSOR, 0, 0))
    scores = lax.all_to_all(scores_own, TENSOR, 0, 0)

    own_residual = lax.dynamic_slice_in_dim(residual, (2 * x_index + z_index) * rows, rows, 0)
    hidden_own = tie(from_z.astype(F32), partial[0, :, :1]) + own_residual.astype(F32)
    hidden_own = (mixed_keep + hidden_own).astype(BF16)

    hidden_z = tie(lax.ppermute(hidden_own, **xor("zh", 2, 1)), scores_own[0, :, :1])
    hidden_0 = jnp.stack([hidden_own, hidden_z])
    hidden_0 = jnp.where(z_index == 0, hidden_0, hidden_0[::-1]).reshape(x_block, width)
    hidden_1 = lax.ppermute(hidden_0, **xor("x", 4, 1))
    hidden_3 = lax.ppermute(hidden_0, **xor("x", 4, 3))

    owner, row_in = positive // rows, positive % rows
    column = (owner % 2 != core).astype(jnp.int32) * half + (owner // 2) * rows + row_in
    t_index = 2 * x_index + z_index
    own_gain = lax.dynamic_slice_in_dim(norm_gain, t_index * feats, feats, 0) / SEQ
    grad_own, grad_give, item_grad, group_rows = softmax_gradient(scores, column, own_gain, users)
    group_rows = lax.all_to_all(group_rows, TENSOR, 0, 0)
    hidden_2 = [
        lax.ppermute(tie(hidden_1[:rows], item_grad[:, :1]), **xor("x", 4, 3)),
        lax.ppermute(tie(hidden_3[rows:], item_grad[:, :1]), **xor("x", 4, 1)),
    ]
    hidden = (hidden_0, hidden_1, *hidden_2, hidden_3)

    other = swap(grad_give)
    losses = jnp.concatenate([part[rows : rows + 3, : heads // 2] for part in (grad_give, other)])
    losses = jnp.pad(losses, ((0, 2), (0, 0)))
    by_plane = plane_payload(item_cache, grad_own, other)
    by_plane = lax.all_to_all(by_plane, PLANE, 0, 0)

    stream = stream_gradient(x_index, group_rows, hidden)

    side = heads // 2
    cut = width // N_P
    attn_give = lax.dynamic_slice_in_dim(attn, (1 - core) * side, side, 1)
    attn_keep = lax.dynamic_slice_in_dim(attn, core * side, side, 1)
    weight_give = swap(dot(stream, attn_give, ((0,), (0,))).astype(BF16))
    weight = dot(stream, attn_keep, ((0,), (0,))) + weight_give.astype(F32)
    weight = weight.astype(BF16).reshape(N_P, cut, side)
    final = jnp.concatenate([weight, jnp.broadcast_to(losses[None], (N_P, 8, side))], axis=1)
    final = lax.all_to_all(final, PLANE, 0, 0)
    head_grad = dot(stream, out_proj, ((1,), (1,))).astype(BF16)
    head_grad = by_xor(head_grad.reshape(4, x_block, heads), x_index).reshape(tokens, heads)
    items_own = by_plane[:, :, :feats].reshape(half, feats)
    by_item = by_plane[:, :, feats:].reshape(N_P, rows, 2, rows).transpose(2, 0, 3, 1)
    by_item = by_item.reshape(2, half, rows)
    user_grad = (
        dot(by_item[0], items_own, ((0,), (0,))) + dot(by_item[1], swap(items_own), ((0,), (0,)))
    ) * LOGIT_SCALE
    weight = jnp.sum(final[:, :cut].astype(F32), axis=0).reshape(2, cut // 2, side)
    weight_keep = lax.dynamic_index_in_dim(weight, core, 0, keepdims=False)
    weight_other = swap(lax.dynamic_index_in_dim(weight, 1 - core, 0, keepdims=False))
    lower = jnp.where(core == 0, weight_keep, weight_other)
    upper = jnp.where(core == 0, weight_other, weight_keep)
    weight_grad = jnp.concatenate([lower, upper], axis=1).T
    loss_mean = jnp.sum(final[:, cut:].astype(F32)) / (2 * half)
    return (loss_mean, item_grad, user_grad, head_grad, weight_grad)


def solution(mesh):
    names, sizes = zip(*AXES)
    fine = Mesh(mesh.devices.reshape(sizes), names)
    both = P(DP, TENSOR)
    return jax.shard_map(
        per_device,
        mesh=fine,
        in_specs=(both, both, P(DP), both, P(DP, None), P(TENSOR, None), P()),
        out_specs=(P(), both, both, both, P(TENSOR, DP)),
        check_vma=False,
    )
```

```python
import jax
import jax.numpy as jnp
from jax import lax
from jax.experimental import pallas as pl
from jax.experimental.pallas import tpu as pltpu
from jax.sharding import Mesh, PartitionSpec as P

BF16 = jnp.bfloat16
F32 = jnp.float32
LOGIT_SCALE = 50.0
NORM_EPS = 1e-06
GROUP = 8
SEQ = 32
AXES = (("zl", 4), ("y", 8), ("c", 2), ("x", 4), ("zh", 2))
TENSOR = ("x", "zh")
PLANE = ("zl", "y")
DP = ("zl", "y", "c")
N_T = 8
N_P = 32


def xor(axis, size, bits):
    return dict(axis_name=axis, perm=[(i, i ^ bits) for i in range(size)])


def swap(value):
    return lax.ppermute(value, **xor("c", 2, 1))


def to_all(value, axes, count):
    return lax.all_to_all(jnp.broadcast_to(value[None], (count,) + value.shape), axes, 0, 0)


def dot(a, b, dims):
    return lax.dot_general(a, b, (dims, ((), ())), preferred_element_type=F32)


def by_xor(value, index):
    parts = [lax.dynamic_slice_in_dim(value, r ^ index, 1, 0) for r in range(value.shape[0])]
    return jnp.concatenate(parts, axis=0)


def tie(value, column):
    return value + (column * 0).astype(value.dtype)


def stream_kernel(x_ref, group_ref, *refs):
    blocks, out_ref, up_ref = refs[:4], refs[4], refs[5]
    width = out_ref.shape[1]
    up_ref[...] = jnp.concatenate([group_ref[t] for t in range(N_T)], axis=1)
    for item in range(GROUP):
        start = item % 2 * SEQ
        tokens = blocks[item // 2][start : start + SEQ, :].astype(F32)
        which = (x_ref[0] ^ (item // 2)) * 2 + item % 2
        up = up_ref[pl.ds(which, 1), :]
        mean = jnp.sum(tokens * tokens, axis=1, keepdims=True) / width
        inverse = lax.rsqrt(mean + NORM_EPS)
        inner = jnp.sum(up * tokens, axis=1, keepdims=True) / width
        stream = inverse * up - tokens * (inverse * inverse * inverse * inner)
        out_ref[item * SEQ : (item + 1) * SEQ, :] = stream.astype(BF16)


def stream_gradient(x_index, group_rows, blocks):
    tokens, width = GROUP * SEQ, blocks[0].shape[1]
    whole = pl.BlockSpec(memory_space=pltpu.VMEM)
    return pl.pallas_call(
        stream_kernel,
        out_shape=jax.ShapeDtypeStruct((tokens, width), BF16),
        in_specs=[pl.BlockSpec(memory_space=pltpu.SMEM)] + [whole] * 5,
        out_specs=whole,
        scratch_shapes=[pltpu.VMEM((GROUP, width), F32)],
        compiler_params=pltpu.CompilerParams(vmem_limit_bytes=24 * 2**20),
        cost_estimate=pl.CostEstimate(
            flops=12 * tokens * width, bytes_accessed=4 * tokens * width, transcendentals=0
        ),
    )(x_index.reshape(1), group_rows, *blocks)


def softmax_kernel(score_ref, column_ref, own_ref, give_ref):
    rows, half = own_ref.shape
    scores = jnp.concatenate([score_ref[t] for t in range(N_T)], axis=1)
    lane = lax.broadcasted_iota(jnp.int32, scores.shape, 1)
    target = column_ref[...] == lane
    top = jnp.max(scores, axis=1, keepdims=True)
    log_total = top + jnp.log(jnp.sum(jnp.exp(scores - top), axis=1, keepdims=True))
    picked = jnp.sum(jnp.where(target, scores, F32(0.0)), axis=1, keepdims=True)
    grad = (jnp.exp(scores - log_total) - target.astype(F32)).astype(BF16)
    own_ref[...] = grad[:, :half]
    give_ref[:rows, :] = grad[:, half:]
    across = lax.broadcasted_iota(jnp.int32, (rows, half), 1)
    down = lax.broadcasted_iota(jnp.int32, (rows, half), 0)
    loss = jnp.where(across == down, log_total - picked, F32(0.0))
    loss = jnp.sum(loss, axis=0, keepdims=True)
    high = loss.astype(BF16).astype(F32)
    middle = (loss - high).astype(BF16).astype(F32)
    low = loss - high - middle
    row = lax.broadcasted_iota(jnp.int32, (16, half), 0)
    terms = jnp.where(row == 0, high, jnp.where(row == 1, middle, low))
    give_ref[rows:, :] = jnp.where(row < 3, terms, F32(0.0)).astype(BF16)


def softmax_gradient(scores, column):
    rows = scores.shape[1]
    half = N_T * scores.shape[2] // 2
    whole = pl.BlockSpec(memory_space=pltpu.VMEM)
    return pl.pallas_call(
        softmax_kernel,
        out_shape=(
            jax.ShapeDtypeStruct((rows, half), BF16),
            jax.ShapeDtypeStruct((rows + 16, half), BF16),
        ),
        in_specs=[whole] * 2,
        out_specs=(whole, whole),
        compiler_params=pltpu.CompilerParams(vmem_limit_bytes=12 * 2**20),
        cost_estimate=pl.CostEstimate(
            flops=16 * rows * half, bytes_accessed=12 * rows * half, transcendentals=4 * rows * half
        ),
    )(scores, column[:, None])


def payload_kernel(item_ref, own_ref, other_ref, out_ref):
    rows, feats = item_ref.shape
    both = jnp.concatenate([own_ref[...].astype(F32), other_ref[:rows, :].astype(F32)], axis=0)
    both = both.T.astype(BF16)
    for place in range(N_P):
        out_ref[place, :, :feats] = item_ref[...]
        out_ref[place, :, feats:] = both[place * rows : (place + 1) * rows, :]


def plane_payload(item_cache, own, other):
    rows, feats = item_cache.shape
    whole = pl.BlockSpec(memory_space=pltpu.VMEM)
    size = N_P * rows * (feats + 2 * rows)
    return pl.pallas_call(
        payload_kernel,
        out_shape=jax.ShapeDtypeStruct((N_P, rows, feats + 2 * rows), BF16),
        in_specs=[whole] * 3,
        out_specs=whole,
        compiler_params=pltpu.CompilerParams(vmem_limit_bytes=12 * 2**20),
        cost_estimate=pl.CostEstimate(flops=0, bytes_accessed=2 * size, transcendentals=0),
    )(item_cache, own, other)


def per_device(item_cache, user_cache, positive, attn_heads, residual, out_proj, norm_gain):
    rows, feats = item_cache.shape
    width = out_proj.shape[1]
    tokens, heads = attn_heads.shape
    half = N_P * rows
    core = lax.axis_index("c")
    x_index = lax.axis_index("x")
    z_index = lax.axis_index("zh")
    x_block = tokens // 4

    attn = by_xor(attn_heads.reshape(4, x_block, heads), x_index).reshape(tokens, heads)
    mixed = dot(attn, out_proj, ((1,), (0,))).astype(BF16)
    from_x = [
        lax.ppermute(mixed[k * x_block : (k + 1) * x_block], **xor("x", 4, k)) for k in (1, 2, 3)
    ]
    mixed_x = mixed[:x_block].astype(F32) + sum(part.astype(F32) for part in from_x)
    mixed_x = mixed_x.reshape(2, rows, width)
    mixed_give = lax.dynamic_index_in_dim(mixed_x, 1 - z_index, 0, keepdims=False)
    mixed_keep = lax.dynamic_index_in_dim(mixed_x, z_index, 0, keepdims=False)
    from_z = lax.ppermute(mixed_give.astype(BF16), **xor("zh", 2, 1))

    users_own = to_all(user_cache, PLANE, N_P).reshape(half, feats)
    users = (users_own, swap(users_own))

    partial = [dot(item_cache, u, ((1,), (1,))) for u in users]
    partial = jnp.concatenate(partial, axis=1)
    share = 2 * half // N_T
    partial = partial.reshape(rows, N_T, share).transpose(1, 0, 2)
    scores_own = jnp.sum(lax.all_to_all(partial, TENSOR, 0, 0), axis=0) * LOGIT_SCALE
    scores = to_all(scores_own, TENSOR, N_T)

    own_residual = lax.dynamic_slice_in_dim(residual, (2 * x_index + z_index) * rows, rows, 0)
    hidden_own = tie(from_z.astype(F32), partial[0, :, :1]) + own_residual.astype(F32)
    hidden_own = (mixed_keep + hidden_own).astype(BF16)

    hidden_z = tie(lax.ppermute(hidden_own, **xor("zh", 2, 1)), scores_own[:, :1])
    hidden_0 = jnp.stack([hidden_own, hidden_z])
    hidden_0 = jnp.where(z_index == 0, hidden_0, hidden_0[::-1]).reshape(x_block, width)
    hidden_1 = lax.ppermute(hidden_0, **xor("x", 4, 1))
    hidden_3 = lax.ppermute(hidden_0, **xor("x", 4, 3))

    owner, row_in = positive // rows, positive % rows
    column = (owner % 2 != core).astype(jnp.int32) * half + (owner // 2) * rows + row_in
    grad_own, grad_give = softmax_gradient(scores, column)
    item_grad = (
        dot(grad_own, users[0], ((1,), (0,))) + dot(grad_give[:rows], users[1], ((1,), (0,)))
    ) * LOGIT_SCALE
    t_index = 2 * x_index + z_index
    own_gain = lax.dynamic_slice_in_dim(norm_gain, t_index * feats, feats, 0) / SEQ
    group_rows = to_all(own_gain[None, :] * item_grad[:GROUP], TENSOR, N_T)
    hidden_2 = lax.ppermute(hidden_0, **xor("x", 4, 2))
    hidden = (hidden_0, hidden_1, hidden_2, hidden_3)

    other = swap(grad_give)
    losses = jnp.concatenate([part[rows : rows + 3, : heads // 2] for part in (grad_give, other)])
    losses = jnp.pad(losses, ((0, 2), (0, 0)))
    near = hidden_1[:rows, :1] + hidden_3[:rows, :1]
    by_plane = plane_payload(tie(item_cache, near), grad_own, other)
    by_plane = lax.all_to_all(by_plane, PLANE, 0, 0)

    stream = stream_gradient(x_index, group_rows, hidden)

    side = heads // 2
    cut = width // N_P
    attn_give = lax.dynamic_slice_in_dim(attn, (1 - core) * side, side, 1)
    attn_keep = lax.dynamic_slice_in_dim(attn, core * side, side, 1)
    weight_give = swap(dot(stream, attn_give, ((0,), (0,))).astype(BF16))
    weight = dot(stream, attn_keep, ((0,), (0,))) + weight_give.astype(F32)
    weight = weight.astype(BF16).reshape(N_P, cut, side)
    final = jnp.concatenate([weight, jnp.broadcast_to(losses[None], (N_P, 8, side))], axis=1)
    final = lax.all_to_all(final, PLANE, 0, 0)
    head_grad = dot(stream, out_proj, ((1,), (1,))).astype(BF16)
    head_grad = by_xor(head_grad.reshape(4, x_block, heads), x_index).reshape(tokens, heads)
    items_own = by_plane[:, :, :feats].reshape(half, feats)
    by_item = by_plane[:, :, feats:].reshape(N_P, rows, 2, rows).transpose(2, 0, 3, 1)
    by_item = by_item.reshape(2, half, rows)
    user_grad = (
        dot(by_item[0], items_own, ((0,), (0,))) + dot(by_item[1], swap(items_own), ((0,), (0,)))
    ) * LOGIT_SCALE
    weight = jnp.sum(final[:, :cut].astype(F32), axis=0).reshape(2, cut // 2, side)
    weight_keep = lax.dynamic_index_in_dim(weight, core, 0, keepdims=False)
    weight_other = swap(lax.dynamic_index_in_dim(weight, 1 - core, 0, keepdims=False))
    lower = jnp.where(core == 0, weight_keep, weight_other)
    upper = jnp.where(core == 0, weight_other, weight_keep)
    weight_grad = jnp.concatenate([lower, upper], axis=1).T
    loss_mean = jnp.sum(final[:, cut:].astype(F32)) / (2 * half)
    return (loss_mean, item_grad, user_grad, head_grad, weight_grad)


def solution(mesh):
    names, sizes = zip(*AXES)
    fine = Mesh(mesh.devices.reshape(sizes), names)
    both = P(DP, TENSOR)
    return jax.shard_map(
        per_device,
        mesh=fine,
        in_specs=(both, both, P(DP), both, P(DP, None), P(TENSOR, None), P()),
        out_specs=(P(), both, both, both, P(TENSOR, DP)),
        check_vma=False,
    )
```

```python
import jax
import jax.numpy as jnp
from jax import lax
from jax.experimental import pallas as pl
from jax.experimental.pallas import tpu as pltpu
from jax.sharding import Mesh, PartitionSpec as P

BF16 = jnp.bfloat16
F32 = jnp.float32
LOGIT_SCALE = 50.0
NORM_EPS = 1e-06
GROUP = 8
SEQ = 32
AXES = (("zl", 4), ("y", 8), ("c", 2), ("x", 4), ("zh", 2))
TENSOR = ("x", "zh")
PLANE = ("zl", "y")
DP = ("zl", "y", "c")
N_T = 8
N_P = 32


def xor(axis, size, bits):
    return dict(axis_name=axis, perm=[(i, i ^ bits) for i in range(size)])


def swap(value):
    return lax.ppermute(value, **xor("c", 2, 1))


def to_all(value, axes, count):
    return lax.all_to_all(jnp.broadcast_to(value[None], (count,) + value.shape), axes, 0, 0)


def dot(a, b, dims):
    return lax.dot_general(a, b, (dims, ((), ())), preferred_element_type=F32)


def by_xor(value, index):
    parts = [lax.dynamic_slice_in_dim(value, r ^ index, 1, 0) for r in range(value.shape[0])]
    return jnp.concatenate(parts, axis=0)


def tie(value, column):
    return value + (column * 0).astype(value.dtype)


def stream_kernel(x_ref, group_ref, *refs):
    first, second, third_0, third_1, fourth, out_ref, up_ref = refs
    halves = (first, first, second, second, third_0, third_1, fourth, fourth)
    width = out_ref.shape[1]
    up_ref[...] = jnp.concatenate([group_ref[t] for t in range(N_T)], axis=1)
    for item in range(GROUP):
        start = 0 if halves[item].shape[0] == SEQ else item % 2 * SEQ
        tokens = halves[item][start : start + SEQ, :].astype(F32)
        which = (x_ref[0] ^ (item // 2)) * 2 + item % 2
        up = up_ref[pl.ds(which, 1), :]
        mean = jnp.sum(tokens * tokens, axis=1, keepdims=True) / width
        inverse = lax.rsqrt(mean + NORM_EPS)
        inner = jnp.sum(up * tokens, axis=1, keepdims=True) / width
        stream = inverse * up - tokens * (inverse * inverse * inverse * inner)
        out_ref[item * SEQ : (item + 1) * SEQ, :] = stream.astype(BF16)


def stream_gradient(x_index, group_rows, blocks):
    tokens, width = GROUP * SEQ, blocks[0].shape[1]
    whole = pl.BlockSpec(memory_space=pltpu.VMEM)
    return pl.pallas_call(
        stream_kernel,
        out_shape=jax.ShapeDtypeStruct((tokens, width), BF16),
        in_specs=[pl.BlockSpec(memory_space=pltpu.SMEM)] + [whole] * 6,
        out_specs=whole,
        scratch_shapes=[pltpu.VMEM((GROUP, width), F32)],
        compiler_params=pltpu.CompilerParams(vmem_limit_bytes=24 * 2**20),
        cost_estimate=pl.CostEstimate(
            flops=12 * tokens * width, bytes_accessed=4 * tokens * width, transcendentals=0
        ),
    )(x_index.reshape(1), group_rows, *blocks)


def score_kernel(part_ref, out_ref):
    total = part_ref[0]
    for t in range(1, N_T):
        total += part_ref[t]
    for t in range(N_T):
        out_ref[t] = total * LOGIT_SCALE


def score_sum(parts):
    whole = pl.BlockSpec(memory_space=pltpu.VMEM)
    return pl.pallas_call(
        score_kernel,
        out_shape=jax.ShapeDtypeStruct(parts.shape, F32),
        in_specs=[whole],
        out_specs=whole,
        compiler_params=pltpu.CompilerParams(vmem_limit_bytes=12 * 2**20),
        cost_estimate=pl.CostEstimate(
            flops=parts.size, bytes_accessed=8 * parts.size, transcendentals=0
        ),
    )(parts)


def softmax_kernel(score_ref, column_ref, own_ref, give_ref):
    rows, half = own_ref.shape
    scores = jnp.concatenate([score_ref[t] for t in range(N_T)], axis=1)
    lane = lax.broadcasted_iota(jnp.int32, scores.shape, 1)
    target = column_ref[...] == lane
    top = jnp.max(scores, axis=1, keepdims=True)
    log_total = top + jnp.log(jnp.sum(jnp.exp(scores - top), axis=1, keepdims=True))
    picked = jnp.sum(jnp.where(target, scores, F32(0.0)), axis=1, keepdims=True)
    grad = (jnp.exp(scores - log_total) - target.astype(F32)).astype(BF16)
    own_ref[...] = grad[:, :half]
    give_ref[:rows, :] = grad[:, half:]
    across = lax.broadcasted_iota(jnp.int32, (rows, half), 1)
    down = lax.broadcasted_iota(jnp.int32, (rows, half), 0)
    loss = jnp.where(across == down, log_total - picked, F32(0.0))
    loss = jnp.sum(loss, axis=0, keepdims=True)
    high = loss.astype(BF16).astype(F32)
    middle = (loss - high).astype(BF16).astype(F32)
    low = loss - high - middle
    row = lax.broadcasted_iota(jnp.int32, (16, half), 0)
    terms = jnp.where(row == 0, high, jnp.where(row == 1, middle, low))
    give_ref[rows:, :] = jnp.where(row < 3, terms, F32(0.0)).astype(BF16)


def softmax_gradient(scores, column):
    rows = scores.shape[1]
    half = N_T * scores.shape[2] // 2
    whole = pl.BlockSpec(memory_space=pltpu.VMEM)
    return pl.pallas_call(
        softmax_kernel,
        out_shape=(
            jax.ShapeDtypeStruct((rows, half), BF16),
            jax.ShapeDtypeStruct((rows + 16, half), BF16),
        ),
        in_specs=[whole] * 2,
        out_specs=(whole, whole),
        compiler_params=pltpu.CompilerParams(vmem_limit_bytes=12 * 2**20),
        cost_estimate=pl.CostEstimate(
            flops=16 * rows * half, bytes_accessed=12 * rows * half, transcendentals=4 * rows * half
        ),
    )(scores, column[:, None])


def payload_kernel(item_ref, own_ref, other_ref, out_ref):
    rows, feats = item_ref.shape
    both = jnp.concatenate([own_ref[...].astype(F32), other_ref[:rows, :].astype(F32)], axis=0)
    both = both.T.astype(BF16)
    for place in range(N_P):
        out_ref[place, :, :feats] = item_ref[...]
        out_ref[place, :, feats:] = both[place * rows : (place + 1) * rows, :]


def plane_payload(item_cache, own, other):
    rows, feats = item_cache.shape
    whole = pl.BlockSpec(memory_space=pltpu.VMEM)
    size = N_P * rows * (feats + 2 * rows)
    return pl.pallas_call(
        payload_kernel,
        out_shape=jax.ShapeDtypeStruct((N_P, rows, feats + 2 * rows), BF16),
        in_specs=[whole] * 3,
        out_specs=whole,
        compiler_params=pltpu.CompilerParams(vmem_limit_bytes=12 * 2**20),
        cost_estimate=pl.CostEstimate(flops=0, bytes_accessed=2 * size, transcendentals=0),
    )(item_cache, own, other)


def per_device(item_cache, user_cache, positive, attn_heads, residual, out_proj, norm_gain):
    rows, feats = item_cache.shape
    width = out_proj.shape[1]
    tokens, heads = attn_heads.shape
    half = N_P * rows
    core = lax.axis_index("c")
    x_index = lax.axis_index("x")
    z_index = lax.axis_index("zh")
    x_block = tokens // 4

    attn = by_xor(attn_heads.reshape(4, x_block, heads), x_index).reshape(tokens, heads)
    mixed = dot(attn, out_proj, ((1,), (0,))).astype(BF16)
    from_x = [
        lax.ppermute(mixed[k * x_block : (k + 1) * x_block], **xor("x", 4, k)) for k in (1, 2, 3)
    ]
    mixed_x = mixed[:x_block].astype(F32) + sum(part.astype(F32) for part in from_x)
    mixed_x = mixed_x.reshape(2, rows, width)
    mixed_give = lax.dynamic_index_in_dim(mixed_x, 1 - z_index, 0, keepdims=False)
    mixed_keep = lax.dynamic_index_in_dim(mixed_x, z_index, 0, keepdims=False)
    from_z = lax.ppermute(mixed_give.astype(BF16), **xor("zh", 2, 1))

    users_own = to_all(user_cache, PLANE, N_P).reshape(half, feats)
    users = (users_own, swap(users_own))

    partial = [dot(item_cache, u, ((1,), (1,))) for u in users]
    partial = jnp.concatenate(partial, axis=1)
    share = 2 * half // N_T
    partial = partial.reshape(rows, N_T, share).transpose(1, 0, 2)
    scores_own = score_sum(lax.all_to_all(partial, TENSOR, 0, 0))
    scores = lax.all_to_all(scores_own, TENSOR, 0, 0)

    own_residual = lax.dynamic_slice_in_dim(residual, (2 * x_index + z_index) * rows, rows, 0)
    hidden_own = tie(from_z.astype(F32), partial[0, :, :1]) + own_residual.astype(F32)
    hidden_own = (mixed_keep + hidden_own).astype(BF16)

    hidden_z = tie(lax.ppermute(hidden_own, **xor("zh", 2, 1)), scores_own[0, :, :1])
    hidden_0 = jnp.stack([hidden_own, hidden_z])
    hidden_0 = jnp.where(z_index == 0, hidden_0, hidden_0[::-1]).reshape(x_block, width)
    hidden_1 = lax.ppermute(hidden_0, **xor("x", 4, 1))
    hidden_3 = lax.ppermute(hidden_0, **xor("x", 4, 3))

    owner, row_in = positive // rows, positive % rows
    column = (owner % 2 != core).astype(jnp.int32) * half + (owner // 2) * rows + row_in
    grad_own, grad_give = softmax_gradient(scores, column)
    item_grad = (
        dot(grad_own, users[0], ((1,), (0,))) + dot(grad_give[:rows], users[1], ((1,), (0,)))
    ) * LOGIT_SCALE
    t_index = 2 * x_index + z_index
    own_gain = lax.dynamic_slice_in_dim(norm_gain, t_index * feats, feats, 0) / SEQ
    group_rows = to_all(own_gain[None, :] * item_grad[:GROUP], TENSOR, N_T)
    hidden_2 = [
        lax.ppermute(tie(hidden_1[:rows], item_grad[:, :1]), **xor("x", 4, 3)),
        lax.ppermute(tie(hidden_3[rows:], item_grad[:, :1]), **xor("x", 4, 1)),
    ]
    hidden = (hidden_0, hidden_1, *hidden_2, hidden_3)

    other = swap(grad_give)
    losses = jnp.concatenate([part[rows : rows + 3, : heads // 2] for part in (grad_give, other)])
    losses = jnp.pad(losses, ((0, 2), (0, 0)))
    by_plane = plane_payload(item_cache, grad_own, other)
    by_plane = lax.all_to_all(by_plane, PLANE, 0, 0)

    stream = stream_gradient(x_index, group_rows, hidden)

    side = heads // 2
    cut = width // N_P
    attn_give = lax.dynamic_slice_in_dim(attn, (1 - core) * side, side, 1)
    attn_keep = lax.dynamic_slice_in_dim(attn, core * side, side, 1)
    weight_give = swap(dot(stream, attn_give, ((0,), (0,))).astype(BF16))
    weight = dot(stream, attn_keep, ((0,), (0,))) + weight_give.astype(F32)
    weight = weight.astype(BF16).reshape(N_P, cut, side)
    final = jnp.concatenate([weight, jnp.broadcast_to(losses[None], (N_P, 8, side))], axis=1)
    final = lax.all_to_all(final, PLANE, 0, 0)
    head_grad = dot(stream, out_proj, ((1,), (1,))).astype(BF16)
    head_grad = by_xor(head_grad.reshape(4, x_block, heads), x_index).reshape(tokens, heads)
    items_own = by_plane[:, :, :feats].reshape(half, feats)
    by_item = by_plane[:, :, feats:].reshape(N_P, rows, 2, rows).transpose(2, 0, 3, 1)
    by_item = by_item.reshape(2, half, rows)
    user_grad = (
        dot(by_item[0], items_own, ((0,), (0,))) + dot(by_item[1], swap(items_own), ((0,), (0,)))
    ) * LOGIT_SCALE
    weight = jnp.sum(final[:, :cut].astype(F32), axis=0).reshape(2, cut // 2, side)
    weight_keep = lax.dynamic_index_in_dim(weight, core, 0, keepdims=False)
    weight_other = swap(lax.dynamic_index_in_dim(weight, 1 - core, 0, keepdims=False))
    lower = jnp.where(core == 0, weight_keep, weight_other)
    upper = jnp.where(core == 0, weight_other, weight_keep)
    weight_grad = jnp.concatenate([lower, upper], axis=1).T
    loss_mean = jnp.sum(final[:, cut:].astype(F32)) / (2 * half)
    return (loss_mean, item_grad, user_grad, head_grad, weight_grad)


def solution(mesh):
    names, sizes = zip(*AXES)
    fine = Mesh(mesh.devices.reshape(sizes), names)
    both = P(DP, TENSOR)
    return jax.shard_map(
        per_device,
        mesh=fine,
        in_specs=(both, both, P(DP), both, P(DP, None), P(TENSOR, None), P()),
        out_specs=(P(), both, both, both, P(TENSOR, DP)),
        check_vma=False,
    )
```
